256 devices in a mesh: mom: 32 (over x, y, z_hi), en: 8 (over z_lo, core).
Axes of the slice: x: 4, y: 4, z: 8 (z_hi: 2, z_lo: 4; z = z_hi * 4 + z_lo), core: 2. Of those that a mesh axis runs over, the one named last changes fastest.
Arguments:
- green: bfloat16 [2, 64, 1024, 256], P(None, 'mom', 'en'), may hold values from 0.0099487305 to 1
- mask: int32 [1024], P('en'), may hold values 0 or 1
- pair_order: int32 [4, 32, 2], P(None, 'mom'), may hold values from 0 to 1, each once within a row
- q_index: int32 [4, 64], P(None, 'mom'), may hold values from 0 to 127
- offsets: int32 [8], replicated, may hold values from 1 to 4, as said below
- occupancy: float32 [8], replicated, may hold values from 0.2 to 4
- coupling: float32 [128, 8], replicated, may hold values from 0.02 to 0.3
Outputs:
- sigma: bfloat16 [2, 64, 1024, 256], P(None, 'mom', 'en')
- polarization: float32 [128, 8, 256], P('mom')
The draws below stay inside these ranges and needn't reach their ends.
Inputs may be any that keep to these rules, and one draw needn't show every extreme that they name: Each row pair_order[r, b] is a permutation of 0 to 1. `offsets`: every branch's offset lies between 1 and 4; some branch has 4 and some has 1.
All inputs are finite; a program needn't handle non-finite values. No bound on the sum of `mask` on one device may be relied on, other than what follows from the above.
Results may differ from the reference program's by a relative error of at most 0.012.
Values may be sent and summed in bfloat16 or wider, within the bound.
No kernel may reach another device: no remote copies, remote signals or barrier semaphores. Data moves between devices by JAX's collectives and lax.ppermute only.
A program may use at most 128 MiB of HBM per device.

```python
import math
import jax
import jax.numpy as jnp
from jax import lax

KD = 2
NORB = 256
MODES = 8
HALO = 4
ROUNDS = 3
KPTS = 64
ENERGIES = 1024
NQ = 128
N_MOM = 32


def draw_offsets(key, part):
    key = jax.random.fold_in(key, 1)
    first, second, third = jax.random.split(key, 3)
    values = jax.random.randint(first, (MODES,), 1, HALO + 1)
    high_at = jax.random.randint(second, (), 0, MODES)
    low_at = (high_at + 1 + jax.random.randint(third, (), 0, MODES - 1)) % MODES
    slots = jnp.arange(MODES)
    values = jnp.where(slots == high_at, HALO, values)
    values = jnp.where(slots == low_at, 1, values)
    return values.astype(jnp.int32)


def with_ends(drawn, key, least, largest):
    dims = drawn.shape
    index_at = [jax.random.randint(jax.random.fold_in(key, axis), (), 0, dims[axis]) for axis in range(len(dims))]
    drawn = drawn.at[tuple(index_at)].set(least)
    longest = dims.index(max(dims))
    index_at[longest] = (index_at[longest] + 1) % dims[longest]
    return drawn.at[tuple(index_at)].set(largest)


def levels(key, shape, cuts, smallest, high):
    def one(dim, parts):
        draws = jax.random.uniform(jax.random.fold_in(jax.random.fold_in(key, 6), dim), (parts,), jnp.float32, smallest / len(cuts), high / len(cuts))
        return jnp.repeat(jnp.exp(draws), shape[dim] // parts).reshape((-1,) + (1,) * (len(shape) - dim - 1))

    level = one(*cuts[0])
    for cut in cuts[1:]:
        level = level * one(*cut)
    return level


def setup_inputs(seed: int = 0) -> dict:
    arg_keys = jax.random.split(jax.random.key(seed), 8)
    return {
        "green": jnp.clip(jnp.exp(math.log(1.0) - 4.61031033 * jax.random.uniform(arg_keys[0], (2, KPTS, ENERGIES, NORB), jnp.float32) ** levels(arg_keys[0], (2, KPTS, ENERGIES, NORB), ((1, 32), (2, 8)), -0.2, 0.2)), 0.0099487305, 1.0).astype(jnp.bfloat16),
        "mask": with_ends((jax.random.randint(arg_keys[1], (ENERGIES,), 0, 4) < 3).astype(jnp.int32), jax.random.fold_in(arg_keys[1], 1), 0, 1),
        "pair_order": jax.vmap(lambda own: jax.random.permutation(own, KD))(jax.random.split(arg_keys[2], (ROUNDS + 1) * N_MOM)).reshape((ROUNDS + 1, N_MOM, KD)).astype(jnp.int32),
        "q_index": with_ends(jax.random.randint(arg_keys[3], (ROUNDS + 1, KPTS), 0, NQ), jax.random.fold_in(arg_keys[3], 1), 0, NQ - 1).astype(jnp.int32),
        "offsets": draw_offsets(jax.random.fold_in(arg_keys[7], 71), 0),
        "occupancy": jnp.clip(jnp.exp(jax.random.uniform(arg_keys[5], (MODES,), jnp.float32, math.log(0.2), math.log(4.0))), 0.2, 4.0),
        "coupling": jnp.clip(jnp.exp(jax.random.uniform(arg_keys[6], (NQ, MODES), jnp.float32, math.log(0.02), math.log(0.3))), 0.02, 0.3),
    }


def pair_terms(own, part_ext, perm, q_row, offsets, occupancy, coupling, mask_row, scale):
    width = own.shape[2]
    rim = (part_ext.shape[2] - width) // 2
    part = jnp.take(part_ext, perm, axis=1)
    onehot = (q_row[:, None] == jnp.arange(coupling.shape[0], dtype=jnp.int32)[None, :]).astype(jnp.float32)
    strength = jnp.dot(onehot, coupling, precision=lax.Precision.HIGHEST, preferred_element_type=jnp.float32)
    weight = mask_row.astype(jnp.float32)[None, :, None]
    less_own = own[0].astype(jnp.float32) * weight
    sig_less = jnp.zeros(own.shape[1:], jnp.float32)
    sig_great = jnp.zeros(own.shape[1:], jnp.float32)
    columns = []
    for mode in range(coupling.shape[1]):
        shift = offsets[mode].astype(jnp.int32)
        above = lax.dynamic_slice_in_dim(part, (rim + shift).astype(jnp.int32), width, 2).astype(jnp.float32)
        below = lax.dynamic_slice_in_dim(part, (rim - shift).astype(jnp.int32), width, 2).astype(jnp.float32)
        occ = occupancy[mode]
        factor = strength[:, mode][:, None, None]
        sig_less = sig_less + factor * ((occ + 1.0) * above[0] + occ * below[0])
        sig_great = sig_great + factor * (occ * above[1] + (occ + 1.0) * below[1])
        columns.append(strength[:, mode][:, None] * jnp.sum(less_own * below[1], axis=1) * scale)
    stacked = jnp.stack(columns, axis=1)
    pol = jnp.einsum("kq,kmo->qmo", onehot, stacked, precision=lax.Precision.HIGHEST)
    return sig_less, sig_great, pol


def reference(green, mask, pair_order, q_index, offsets, occupancy, coupling):
    extended = jnp.pad(green, ((0, 0), (0, 0), (HALO, HALO), (0, 0)))
    blocks = extended.reshape(2, N_MOM, KD, ENERGIES + 2 * HALO, NORB)
    scale = 1.0 / ENERGIES

    def device(index):
        own_ext = blocks[:, index]
        own = own_ext[:, :, HALO:HALO + ENERGIES]
        total_less = jnp.zeros((KD, ENERGIES, NORB), jnp.float32)
        total_great = jnp.zeros((KD, ENERGIES, NORB), jnp.float32)
        pol = jnp.zeros((NQ, MODES, NORB), jnp.float32)
        for rnd in range(ROUNDS + 1):
            if rnd == 0:
                part = own_ext
            else:
                part = blocks[:, jnp.bitwise_xor(index, jnp.int32(1 << (rnd - 1)))]
            perm = pair_order[rnd, index]
            q_row = lax.dynamic_slice_in_dim(q_index[rnd], (index * KD).astype(jnp.int32), KD)
            less, great, term = pair_terms(own, part, perm, q_row, offsets, occupancy, coupling, mask, scale)
            total_less = total_less + less
            total_great = total_great + great
            pol = pol + term
        weight = mask.astype(jnp.float32)[None, :, None]
        sig = jnp.stack([total_less * weight, total_great * weight]).astype(jnp.bfloat16)
        return sig, pol

    sig, pols = lax.map(device, jnp.arange(N_MOM, dtype=jnp.int32))
    sig = jnp.transpose(sig, (1, 0, 2, 3, 4)).reshape(2, KPTS, ENERGIES, NORB)
    return sig, jnp.sum(pols, axis=0)
```

```python
import jax
import jax.numpy as jnp
from jax import lax
from jax.experimental import pallas as pl
from jax.experimental.pallas import tpu as pltpu
from jax.sharding import Mesh, PartitionSpec as P

HALO = 4
AXES = ("x", "y", "zh", "zl", "c")
F32 = jnp.float32
BF16 = jnp.bfloat16
HIGHEST = lax.Precision.HIGHEST
SMEM = pl.BlockSpec(memory_space=pltpu.SMEM)
LIMIT = 48 * 1024 * 1024


def iota(shape, dim):
    return lax.broadcasted_iota(jnp.int32, shape, dim)


def dot(a, b, precision=None):
    return lax.dot_general(
        a, b, (((1,), (0,)), ((), ())), precision=precision, preferred_element_type=F32
    )


def band(dif, above, below):
    out = jnp.zeros(dif.shape, F32)
    for d in range(1, HALO + 1):
        out = jnp.where(dif == d, above[d - 1], out)
        out = jnp.where(dif == -d, below[d - 1], out)
    return out


def pair_products(great, shifted, k):
    great = great.astype(F32)
    return [
        jnp.sum(great * shifted[k * HALO + d].astype(F32), axis=0, keepdims=True)
        for d in range(HALO)
    ]


def prepare_kernel(
    order, q_row, offsets, occupancy, coupling, mask, green, rim, main, edge, place, onehot, shifted, first
):
    width = mask.shape[1]
    modes = coupling.shape[0]
    pairs = q_row.shape[0] * q_row.shape[1]
    kd = q_row.shape[1]
    q_of = [q_row[p // kd, p % kd] for p in range(pairs)]

    q_col = jnp.zeros((pairs, coupling.shape[1]), jnp.int32)
    for p in range(pairs):
        q_col = jnp.where(iota(q_col.shape, 0) == p, q_of[p], q_col)
    chosen = (q_col == iota(q_col.shape, 1)).astype(F32)
    strength = lax.dot_general(
        chosen, coupling[...], (((1,), (1,)), ((), ())), precision=HIGHEST, preferred_element_type=F32
    )
    off_col = jnp.zeros((modes, width), jnp.int32)
    occ_col = jnp.zeros((modes, width), F32)
    for m in range(modes):
        off_col = jnp.where(iota(off_col.shape, 0) == m, offsets[m], off_col)
        occ_col = jnp.where(iota(off_col.shape, 0) == m, occupancy[m], occ_col)
    emit, absorb = [], []
    for d in range(1, HALO + 1):
        emit.append(dot(strength, jnp.where(off_col == d, occ_col + 1.0, 0.0), HIGHEST))
        absorb.append(dot(strength, jnp.where(off_col == d, occ_col, 0.0), HIGHEST))

    row, col = iota((width, width), 0), iota((width, width), 1)
    active = jnp.sum(jnp.where(row == col, mask[...], 0).astype(F32), axis=1, keepdims=True)
    live = jnp.where(active > 0.0, col - row, 2 * width)
    rows = iota((8 * HALO, 2 * 16), 0)
    cols = iota((8 * HALO, 2 * 16), 1)
    source = jnp.where(cols < 16, cols, cols + (width - 32))
    step = rows % HALO
    target = jnp.where(rows < 4 * HALO, width + step, step - HALO)
    part_of = (rows // HALO) % 4
    for comp in range(2):
        for k in range(kd):
            ck = comp * kd + k
            edges = []
            for r in range(pairs // kd):
                p = r * kd + k
                up = [x[p : p + 1, :] for x in emit]
                down = [x[p : p + 1, :] for x in absorb]
                if comp == 1:
                    up, down = down, up
                main[ck, :, r * width : (r + 1) * width] = band(live, up, down).astype(BF16)
                dif = jnp.where(part_of == ck, source - target, 2 * width)
                edges.append(band(dif, [x[:, :32] for x in up], [x[:, :32] for x in down]))
            edge[ck] = jnp.concatenate(edges, axis=1).astype(BF16)
            spot = iota((width, 32), 1)
            to = jnp.where(spot < 16, spot % HALO, width - HALO + spot % HALO)
            hit = (to == iota((width, 32), 0)) & ((spot // HALO) % 4 == ck) & (active > 0.0)
            place[ck] = hit.astype(F32).astype(BF16)

    goal = jnp.zeros((1, pairs * HALO), jnp.int32)
    lane = iota(goal.shape, 1)
    for p in range(pairs):
        goal = jnp.where(lane // HALO == p, q_of[p] * HALO + lane % HALO, goal)
    onehot[...] = (iota(onehot.shape, 0) == goal).astype(F32).astype(BF16)

    weights = jnp.broadcast_to(mask[...], (width, width)).astype(F32)
    for d in range(1, HALO + 1):
        move = jnp.where(col == row + d, weights, 0.0).astype(BF16)
        edge_row, edge_col = iota((width, 16), 0), iota((width, 16), 1)
        wrap = (edge_col + width == edge_row + d).astype(F32).astype(BF16)
        for k in range(kd):
            moved = dot(move, green[0, k]) + dot(wrap, rim[k])
            shifted[k * HALO + d - 1] = moved.astype(BF16)
    lines = []
    for k in range(kd):
        lines += pair_products(green[1, order[0, k]], shifted, k)
    first[...] = jnp.concatenate(lines, axis=0)


def prepare(order, q_row, offsets, occupancy, coupling, mask, green, rim):
    _, kd, width, norb = green.shape
    pairs = q_row.shape[0] * kd
    modes, nq = coupling.shape
    rounds = q_row.shape[0]
    vmem = pl.BlockSpec(memory_space=pltpu.VMEM)
    return pl.pallas_call(
        prepare_kernel,
        out_shape=(
            jax.ShapeDtypeStruct((2 * kd, width, rounds * width), BF16),
            jax.ShapeDtypeStruct((2 * kd, 32, rounds * 32), BF16),
            jax.ShapeDtypeStruct((2 * kd, width, 32), BF16),
            jax.ShapeDtypeStruct((nq * HALO, pairs * HALO), BF16),
            jax.ShapeDtypeStruct((kd * HALO, width, norb), BF16),
            jax.ShapeDtypeStruct((kd * HALO, norb), F32),
        ),
        in_specs=[SMEM, SMEM, SMEM, SMEM, vmem, vmem, vmem, vmem],
        out_specs=(vmem,) * 6,
        compiler_params=pltpu.CompilerParams(vmem_limit_bytes=LIMIT),
        cost_estimate=pl.CostEstimate(flops=2**20, bytes_accessed=2**21, transcendentals=0),
        name="prepare",
    )(order, q_row, offsets, occupancy, coupling, mask, green, rim)


def terms_kernel(order, far, near, next_near, shifted, first, onehot, out):
    lines = [first[...]]
    kd = far.shape[0]
    for r, ref in ((1, far), (2, near), (3, next_near)):
        for k in range(kd):
            index = order[r, k]
            great = ref[index] if r == 1 else ref[0, index]
            lines += pair_products(great, shifted, k)
    terms = jnp.concatenate(lines, axis=0).astype(BF16)
    out[...] = dot(onehot[...], terms).astype(BF16)


def terms(order, far, near, next_near, shifted, first, onehot):
    _, kd, width, norb = near.shape
    vmem = pl.BlockSpec(memory_space=pltpu.VMEM)
    great = pl.BlockSpec((1, kd, width, norb), lambda i: (1, 0, 0, 0))
    return pl.pallas_call(
        terms_kernel,
        grid=(1,),
        out_shape=jax.ShapeDtypeStruct((onehot.shape[0], norb), BF16),
        in_specs=[SMEM, vmem, great, great, vmem, vmem, vmem],
        out_specs=vmem,
        compiler_params=pltpu.CompilerParams(vmem_limit_bytes=LIMIT),
        cost_estimate=pl.CostEstimate(flops=2**20, bytes_accessed=2**20, transcendentals=0),
        name="terms",
    )(order, far, near, next_near, shifted, first, onehot)


def column_kernel(
    order, place, got, edge, own_t, own_b, less_t, less_b, great_t, great_b, near_t, near_b, next_t, next_b, out
):
    total = jnp.sum(got[...].astype(F32), axis=0)
    half = total.shape[0] // 2
    count = out.shape[0] // 2
    for dest in range(out.shape[0]):
        at = (dest // count) * half
        out[dest, :half] = total[at : at + half].astype(BF16)
        out[dest, half:] = jnp.zeros((out.shape[1] - half, out.shape[2]), BF16)
    kd = less_t.shape[0]
    moved = jnp.zeros((32, out.shape[2]), F32)
    for comp in range(2):
        far_t, far_b = (less_t, less_b) if comp == 0 else (great_t, great_b)
        for k in range(kd):
            parts = []
            for r, (top, bottom) in enumerate(
                ((own_t, own_b), (far_t, far_b), (near_t, near_b), (next_t, next_b))
            ):
                index = order[r, k]
                if r == 1:
                    parts += [top[index], bottom[index]]
                else:
                    parts += [top[comp, index], bottom[comp, index]]
            moved = moved + dot(edge[comp * kd + k], jnp.concatenate(parts, axis=0))
    block = place[0]
    me = place[1]

    @pl.when(me < count - 1)
    def _():
        out[block * count + me + 1, half:] = moved[:16].astype(BF16)

    @pl.when(me > 0)
    def _():
        out[block * count + me - 1, half:] = moved[16:].astype(BF16)


def column(order, place, got, edge, own, less, great, near, next_near):
    _, kd, width, norb = own.shape
    vmem = pl.BlockSpec(memory_space=pltpu.VMEM)
    last = width // 16 - 1
    top4 = pl.BlockSpec((2, kd, 16, norb), lambda i: (0, 0, 0, 0))
    low4 = pl.BlockSpec((2, kd, 16, norb), lambda i: (0, 0, last, 0))
    top3 = pl.BlockSpec((kd, 16, norb), lambda i: (0, 0, 0))
    low3 = pl.BlockSpec((kd, 16, norb), lambda i: (0, last, 0))
    return pl.pallas_call(
        column_kernel,
        grid=(1,),
        out_shape=jax.ShapeDtypeStruct((16, 32, norb), BF16),
        in_specs=[SMEM, SMEM, vmem, vmem, top4, low4, top3, low3, top3, low3, top4, low4, top4, low4],
        out_specs=vmem,
        compiler_params=pltpu.CompilerParams(vmem_limit_bytes=LIMIT),
        cost_estimate=pl.CostEstimate(flops=2**20, bytes_accessed=2**20, transcendentals=0),
        name="column",
    )(order, place, got, edge, own, own, less, less, great, great, near, near, next_near, next_near)


def finish_kernel(
    order, place, offsets, coupling, got, main, spots, own, less, great, near, next_near, sigma, pol, total
):
    kd = less.shape[0]
    half = got.shape[1] // 2
    count = got.shape[0] // 2
    me = place[1]
    base = place[0] * count
    before = got[base + jnp.maximum(me - 1, 0), half:]
    after = got[base + jnp.minimum(me + 1, count - 1), half:]
    before = jnp.where(me > 0, before.astype(F32), 0.0).astype(BF16)
    after = jnp.where(me < count - 1, after.astype(F32), 0.0).astype(BF16)
    rims = jnp.concatenate([before, after], axis=0)
    for comp in range(2):
        far = less if comp == 0 else great
        for k in range(kd):
            ck = comp * kd + k
            blocks = [own[comp, order[0, k]], far[order[1, k]]]
            blocks += [near[comp, order[2, k]], next_near[comp, order[3, k]]]
            acc = dot(main[ck], jnp.concatenate(blocks, axis=0)) + dot(spots[ck], rims)
            sigma[comp, k] = acc.astype(BF16)
    total[...] = jnp.sum(got[:, :half].astype(F32), axis=0)
    scale = place[2].astype(F32)
    scale = 1.0 / scale
    for j in range(pol.shape[0]):
        for m in range(pol.shape[1]):
            factor = coupling[m, place[3] + j] * scale
            pol[j, m : m + 1, :] = factor * total[pl.ds(j * HALO + offsets[m] - 1, 1), :]


def finish(order, place, offsets, coupling, got, main, spots, own, less, great, near, next_near, owned):
    norb = own.shape[3]
    vmem = pl.BlockSpec(memory_space=pltpu.VMEM)
    return pl.pallas_call(
        finish_kernel,
        out_shape=(
            jax.ShapeDtypeStruct(own.shape, BF16),
            jax.ShapeDtypeStruct((owned, coupling.shape[0], norb), F32),
        ),
        in_specs=[SMEM] * 4 + [vmem] * 8,
        out_specs=(vmem, vmem),
        scratch_shapes=[pltpu.VMEM((got.shape[1] // 2, norb), F32)],
        compiler_params=pltpu.CompilerParams(vmem_limit_bytes=LIMIT),
        cost_estimate=pl.CostEstimate(flops=2**24, bytes_accessed=2**21, transcendentals=0),
        name="finish",
    )(order, place, offsets, coupling, got, main, spots, own, less, great, near, next_near)


def on_device(green, mask, pair_order, q_index, offsets, occupancy, coupling):
    _, kd, width, norb = green.shape
    count = lax.axis_size(("zl", "c"))
    owned = coupling.shape[0] // lax.axis_size(("x", "y", "zh"))
    order = pair_order[:, 0]
    spread = coupling.T
    place = jnp.stack(
        [
            lax.axis_index("zh"),
            lax.axis_index(("zl", "c")),
            width * count,
            lax.axis_index(("x", "y", "zh")) * owned,
        ]
    ).astype(jnp.int32)

    swap = [(0, 1), (1, 0)]
    great = lax.ppermute(green[1], "zh", swap)
    rim = green[0, :, :16] * mask[None, :16, None].astype(BF16)
    rim = lax.ppermute(rim, ("zl", "c"), [(i + 1, i) for i in range(count - 1)])
    near = lax.ppermute(green, "y", [(i, i ^ 1) for i in range(4)])
    next_near = lax.ppermute(green, "y", [(i, i ^ 2) for i in range(4)])
    main, edge, spots, onehot, shifted, first = prepare(
        order, q_index, offsets, occupancy, spread, mask[None, :], green, rim
    )
    held, first = lax.optimization_barrier((green[0], first))
    less = lax.ppermute(held, "zh", swap)

    dense = terms(order, great, near, next_near, shifted, first, onehot)
    got = lax.all_to_all(dense.reshape(16, -1, norb), ("x", "y"), 0, 0, tiled=True)
    sent = column(order, place, got, edge, green, less, great, near, next_near)
    got = lax.all_to_all(sent, ("zh", "zl", "c"), 0, 0, tiled=True)
    return finish(
        order, place, offsets, spread, got, main, spots, green, less, great, near, next_near, owned
    )


def solution(mesh):
    split = Mesh(mesh.devices.reshape(4, 4, 2, 4, 2), AXES)
    mom, en = ("x", "y", "zh"), ("zl", "c")
    in_specs = (P(None, mom, en, None), P(en), P(None, mom, None), P(None, mom), P(), P(), P())
    out_specs = (P(None, mom, en, None), P(mom, None, None))
    return jax.shard_map(
        on_device, mesh=split, in_specs=in_specs, out_specs=out_specs, check_vma=False
    )
```

```python
import functools

import jax
import jax.numpy as jnp
from jax import lax
from jax.experimental import pallas as pl
from jax.experimental.pallas import tpu as pltpu
from jax.sharding import Mesh, PartitionSpec as P

HALO = 4
AXES = ("x", "y", "zh", "zl", "c")
F32 = jnp.float32
BF16 = jnp.bfloat16
HIGHEST = lax.Precision.HIGHEST
SMEM = pl.BlockSpec(memory_space=pltpu.SMEM)
LIMIT = 40 * 1024 * 1024
VMEM = pl.BlockSpec(memory_space=pltpu.VMEM)


def iota(shape, dim):
    return lax.broadcasted_iota(jnp.int32, shape, dim)


def dot(a, b, precision=None):
    return lax.dot_general(
        a, b, (((1,), (0,)), ((), ())), precision=precision, preferred_element_type=F32
    )


def band(dif, above, below):
    out = jnp.zeros(dif.shape, F32)
    for d in range(1, HALO + 1):
        out = jnp.where(dif == d, above[d - 1], out)
        out = jnp.where(dif == -d, below[d - 1], out)
    return out


def pair_products(great, shifted, k):
    great = great.astype(F32)
    return [
        jnp.sum(great * shifted[k * HALO + d].astype(F32), axis=0, keepdims=True)
        for d in range(HALO)
    ]


def call(kernel, name, outs, specs, args, scratch=(), flops=2**20):
    return pl.pallas_call(
        kernel,
        out_shape=outs,
        in_specs=specs,
        out_specs=jax.tree.map(lambda _: VMEM, outs),
        scratch_shapes=scratch,
        compiler_params=pltpu.CompilerParams(vmem_limit_bytes=LIMIT),
        cost_estimate=pl.CostEstimate(flops=flops, bytes_accessed=2**20, transcendentals=0),
        name=name,
    )(*args)


def shape(*dims, dtype=BF16):
    return jax.ShapeDtypeStruct(dims, dtype)


def shift_kernel(order, q_row, mask, green, onehot, shifted, first):
    kd, rounds = order.shape
    width = mask.shape[1]
    goal = jnp.zeros((1, onehot.shape[1]), jnp.int32)
    lane = iota(goal.shape, 1)
    for p in range(rounds * kd):
        goal = jnp.where(lane // HALO == p, q_row[p % kd, p // kd] * HALO + lane % HALO, goal)
    onehot[...] = (iota(onehot.shape, 0) == goal).astype(F32).astype(BF16)

    row, col = iota((width, width), 0), iota((width, width), 1)
    weights = jnp.broadcast_to(mask[...], (width, width)).astype(F32)
    for d in range(1, HALO + 1):
        move = jnp.where(col == row + d, weights, 0.0).astype(BF16)
        for k in range(kd):
            shifted[k * HALO + d - 1] = dot(move, green[0, k]).astype(BF16)
    lines = []
    for k in range(kd):
        lines += pair_products(green[1, order[k, 0]], shifted, k)
    first[...] = jnp.concatenate(lines, axis=0)


def tail_kernel(order, green, shifted, rim, first, tail, total):
    kd, width = green.shape[1:3]
    rows, cols = iota((16, 16), 0), iota((16, 16), 1)
    lines = []
    for k in range(kd):
        last = green[1, order[k, 0], width - 16 :].astype(F32)
        for d in range(1, HALO + 1):
            wrap = (cols + 16 == rows + d).astype(F32).astype(BF16)
            at = k * HALO + d - 1
            moved = dot(wrap, rim[k])
            tail[at] = (shifted[at, width - 16 :].astype(F32) + moved).astype(BF16)
            lines.append(jnp.sum(last * moved, axis=0, keepdims=True))
    total[...] = first[...] + jnp.concatenate(lines, axis=0)


def terms_kernel(order, far, near, next_near, shifted, tail, first, onehot, out):
    lines = [first[...]]
    kd, width, _ = far.shape
    for r, ref in ((1, far), (2, near), (3, next_near)):
        for k in range(kd):
            great = ref[order[k, r]].astype(F32)
            for d in range(HALO):
                at = k * HALO + d
                body = great[: width - 16] * shifted[at, : width - 16].astype(F32)
                end = great[width - 16 :] * tail[at].astype(F32)
                lines.append(
                    jnp.sum(body, axis=0, keepdims=True) + jnp.sum(end, axis=0, keepdims=True)
                )
    terms = jnp.concatenate(lines, axis=0).astype(BF16)
    out[...] = dot(onehot[...], terms).astype(BF16)


def column_kernel(got, out):
    total = jnp.sum(got[...].astype(F32), axis=0).astype(BF16)
    half = out.shape[1]
    for dest in range(out.shape[0]):
        at = (dest // (out.shape[0] // 2)) * half
        out[dest] = total[at : at + half]


def weights_kernel(q_row, place, offsets, occupancy, coupling, mask, main, edge, owner, *, scale):
    kd, rounds = q_row.shape
    width = mask.shape[1]
    modes = coupling.shape[0]
    pairs = rounds * kd

    q_col = jnp.zeros((pairs, coupling.shape[1]), jnp.int32)
    for p in range(pairs):
        q_col = jnp.where(iota(q_col.shape, 0) == p, q_row[p % kd, p // kd], q_col)
    chosen = (q_col == iota(q_col.shape, 1)).astype(F32)
    strength = lax.dot_general(
        chosen, coupling[...], (((1,), (1,)), ((), ())), precision=HIGHEST, preferred_element_type=F32
    )
    off_col = jnp.zeros((modes, width), jnp.int32)
    occ_col = jnp.zeros((modes, width), F32)
    for m in range(modes):
        off_col = jnp.where(iota(off_col.shape, 0) == m, offsets[m], off_col)
        occ_col = jnp.where(iota(off_col.shape, 0) == m, occupancy[m], occ_col)
    emit, absorb = [], []
    for d in range(1, HALO + 1):
        emit.append(dot(strength, jnp.where(off_col == d, occ_col + 1.0, 0.0), HIGHEST))
        absorb.append(dot(strength, jnp.where(off_col == d, occ_col, 0.0), HIGHEST))

    rows, cols = iota(owner.shape, 0), iota(owner.shape, 1)
    wide = (owner.shape[0], coupling.shape[1])
    mine = (iota(wide, 1) == place[0] + iota(wide, 0) // modes).astype(F32)
    factor = lax.dot_general(
        mine, coupling[...], (((1,), (1,)), ((), ())), precision=HIGHEST, preferred_element_type=F32
    )
    branch = iota(factor.shape, 1) == iota(factor.shape, 0) % modes
    factor = jnp.sum(jnp.where(branch, factor, 0.0), axis=1, keepdims=True) * scale
    off = jnp.zeros(owner.shape, jnp.int32)
    for m in range(modes):
        off = jnp.where(rows % modes == m, offsets[m], off)
    hit = (rows // modes == cols // HALO) & (off == cols % HALO + 1)
    owner[...] = jnp.where(hit, factor, 0.0)

    row, col = iota((width, width), 0), iota((width, width), 1)
    active = jnp.sum(jnp.where(row == col, mask[...], 0).astype(F32), axis=1, keepdims=True)
    live = jnp.where(active > 0.0, col - row, 2 * width)
    rows, cols = iota((32, 32), 0), iota((32, 32), 1)
    source = jnp.where(cols < 16, cols, cols + (width - 32))
    target = jnp.where(rows < 16, width + rows % HALO, rows % HALO - HALO)
    part_of = (rows // HALO) % 4
    for comp in range(2):
        for k in range(kd):
            ck = comp * kd + k
            dif = jnp.where(part_of == ck, source - target, 2 * width)
            edges = []
            for r in range(rounds):
                p = r * kd + k
                up = [x[p : p + 1, :] for x in emit]
                down = [x[p : p + 1, :] for x in absorb]
                if comp == 1:
                    up, down = down, up
                main[ck, :, r * width : (r + 1) * width] = band(live, up, down).astype(BF16)
                edges.append(band(dif, [x[:, :32] for x in up], [x[:, :32] for x in down]))
            edge[ck] = jnp.concatenate(edges, axis=1).astype(BF16)


def sigma_kernel(
    order, place, main, edge, own, less1, less2, less3, great1, great2, great3, _after,
    sigma, rims, core_edge, chip_edge
):
    kd, rounds = order.shape
    width = own.shape[2]
    moved = jnp.zeros((32, own.shape[3]), F32)
    for comp in range(2):
        for k in range(kd):
            ck = comp * kd + k
            others = (less1, less2, less3) if comp == 0 else (great1, great2, great3)
            blocks = [own[comp, order[k, 0]]]
            blocks += [x[order[k, r + 1]] for r, x in enumerate(others)]
            ends = []
            for x in blocks:
                ends += [x[:16], x[width - 16 :]]
            acc = dot(main[ck], jnp.concatenate(blocks, axis=0))
            sigma[comp, k] = acc.astype(BF16)
            rims[ck, :16] = acc[:16]
            rims[ck, 16:] = acc[width - 16 :]
            moved = moved + dot(edge[ck], jnp.concatenate(ends, axis=0))
    first_core = jnp.broadcast_to(place[1], (16, moved.shape[1])) == 0
    core_edge[...] = jnp.where(first_core, moved[:16], moved[16:]).astype(BF16)
    chip_edge[...] = jnp.where(first_core, moved[16:], moved[:16]).astype(BF16)


def rim_kernel(place, mask, rims, core_edge, chip_edge, _, sigma):
    kd = sigma.shape[1]
    width = mask.shape[1]
    step = pl.program_id(0)
    from_core = jnp.broadcast_to(place[1] ^ step, core_edge.shape) == 1
    edge = jnp.where(from_core, core_edge[...].astype(F32), chip_edge[...].astype(F32)).astype(BF16)
    at = iota((16, width), 0) + step * (width - 16)
    active = jnp.sum(
        jnp.where(at == iota((16, width), 1), mask[...], 0).astype(F32), axis=1, keepdims=True
    )
    rows, cols = iota((16, 16), 0), iota((16, 16), 1)
    to = cols % HALO + step * (16 - HALO)
    for comp in range(2):
        for k in range(kd):
            ck = comp * kd + k
            hit = (rows == to) & (cols // HALO == ck) & (active > 0.0)
            total = rims[ck, pl.ds(step * 16, 16)] + dot(hit.astype(F32).astype(BF16), edge)
            sigma[comp, k] = total.astype(BF16)


def add_rims(place, mask, rims, core_edge, chip_edge, sigma):
    _, kd, width, norb = sigma.shape
    last = width // 16 - 1
    return pl.pallas_call(
        rim_kernel,
        grid=(2,),
        out_shape=shape(*sigma.shape),
        in_specs=[SMEM] + [VMEM] * 4 + [pl.BlockSpec(memory_space=pl.ANY)],
        out_specs=pl.BlockSpec((2, kd, 16, norb), lambda i: (0, 0, i * last, 0)),
        input_output_aliases={5: 0},
        compiler_params=pltpu.CompilerParams(vmem_limit_bytes=LIMIT),
        cost_estimate=pl.CostEstimate(flops=2**20, bytes_accessed=2**20, transcendentals=0),
        name="rims",
    )(place, mask, rims, core_edge, chip_edge, sigma)


def owner_kernel(got, owner, pol):
    total = jnp.sum(got[...].astype(F32), axis=0)
    pol[...] = dot(owner[...], total, HIGHEST)


def tie(x, y):
    return lax.optimization_barrier((x, y))[0]


def on_device(green, mask, pair_order, q_index, offsets, occupancy, coupling):
    _, kd, width, norb = green.shape
    rounds = pair_order.shape[0]
    count = lax.axis_size(("zl", "c"))
    owned = coupling.shape[0] // lax.axis_size(("x", "y", "zh"))
    order, q_row, spread, mask_row = pair_order[:, 0].T, q_index.T, coupling.T, mask[None, :]
    place = [lax.axis_index(("x", "y", "zh")) * owned, lax.axis_index("c")]
    place = jnp.stack([jnp.asarray(x, jnp.int32) for x in place])

    swap = [(0, 1), (1, 0)]

    def exchange(x):
        near = lax.ppermute(x, "y", [(i, i ^ 1) for i in range(4)])
        next_near = lax.ppermute(x, "y", [(i, i ^ 2) for i in range(4)])
        return lax.ppermute(x, "zh", swap), near, next_near

    great = exchange(green[1])
    rim = green[0, :, :16] * mask[None, :16, None].astype(BF16)
    rim = lax.ppermute(rim, ("zl", "c"), [(i + 1, i) for i in range(count - 1)])
    main, edge, owner = call(
        functools.partial(weights_kernel, scale=1.0 / (width * count)),
        "weights",
        (
            shape(2 * kd, width, rounds * width),
            shape(2 * kd, 32, rounds * 32),
            shape(owned * offsets.shape[0], owned * HALO, dtype=F32),
        ),
        [SMEM] * 4 + [VMEM] * 2,
        (q_row, place, offsets, occupancy, spread, mask_row),
    )
    onehot, shifted, first = call(
        shift_kernel,
        "shift",
        (
            shape(coupling.shape[0] * HALO, rounds * kd * HALO),
            shape(kd * HALO, width, norb),
            shape(kd * HALO, norb, dtype=F32),
        ),
        [SMEM, SMEM, VMEM, VMEM],
        (order, q_row, mask_row, green),
    )
    tail, first = call(
        tail_kernel,
        "tail",
        (shape(kd * HALO, 16, norb), shape(*first.shape, dtype=F32)),
        [SMEM] + [VMEM] * 4,
        (order, green, shifted, rim, first),
    )
    dense = call(
        terms_kernel,
        "terms",
        shape(onehot.shape[0], norb),
        [SMEM] + [VMEM] * 7,
        (order, *great, tie(shifted, main), tail, first, onehot),
    )
    less = exchange(tie(green[0], dense))
    got = lax.all_to_all(dense.reshape(16, -1, norb), ("x", "y"), 0, 0, tiled=True)
    sent = call(
        column_kernel, "column", shape(2 * count, owned * HALO, norb), [VMEM], (got,)
    )
    got = lax.all_to_all(sent, ("zh", "zl", "c"), 0, 0, tiled=True)
    sigma, rims, core_edge, chip_edge = call(
        sigma_kernel,
        "sigma",
        (
            shape(*green.shape),
            shape(2 * kd, 32, norb, dtype=F32),
            shape(2 * kd * HALO, norb),
            shape(2 * kd * HALO, norb),
        ),
        [SMEM] * 2 + [VMEM] * 9 + [pl.BlockSpec(memory_space=pl.ANY)],
        (order, place, main, edge, green, *less, *great, sent),
        flops=2**34,
    )
    from_core = lax.ppermute(core_edge, "c", swap)
    meet = [(i, i + 1) for i in range(1, count - 1, 2)]
    from_chip = lax.ppermute(chip_edge, ("zl", "c"), meet + [(j, i) for i, j in meet])
    sigma = add_rims(place, mask_row, rims, from_core, from_chip, sigma)

    pol = call(
        owner_kernel,
        "owner",
        shape(owner.shape[0], norb, dtype=F32),
        [VMEM] * 2,
        (got, owner),
    )
    return sigma, pol.reshape(owned, -1, norb)


def solution(mesh):
    split = Mesh(mesh.devices.reshape(4, 4, 2, 4, 2), AXES)
    mom, en = ("x", "y", "zh"), ("zl", "c")
    in_specs = (P(None, mom, en, None), P(en), P(None, mom, None), P(None, mom), P(), P(), P())
    out_specs = (P(None, mom, en, None), P(mom, None, None))
    return jax.shard_map(
        on_device, mesh=split, in_specs=in_specs, out_specs=out_specs, check_vma=False
    )
```

```python
import functools

import jax
import jax.numpy as jnp
from jax import lax
from jax.experimental import pallas as pl
from jax.experimental.pallas import tpu as pltpu
from jax.sharding import Mesh, PartitionSpec as P

HALO = 4
AXES = ("x", "y", "zh", "zl", "c")
F32 = jnp.float32
BF16 = jnp.bfloat16
HIGHEST = lax.Precision.HIGHEST
SMEM = pl.BlockSpec(memory_space=pltpu.SMEM)
LIMIT = 12 * 1024 * 1024
VMEM = pl.BlockSpec(memory_space=pltpu.VMEM)


def iota(shape, dim):
    return lax.broadcasted_iota(jnp.int32, shape, dim)


def dot(a, b, precision=None):
    return lax.dot_general(
        a, b, (((1,), (0,)), ((), ())), precision=precision, preferred_element_type=F32
    )


def band(dif, above, below):
    out = jnp.zeros(dif.shape, F32)
    for d in range(1, HALO + 1):
        out = jnp.where(dif == d, above[d - 1], out)
        out = jnp.where(dif == -d, below[d - 1], out)
    return out


def pair_products(great, shifted, k):
    great = great.astype(F32)
    return [
        jnp.sum(great * shifted[k * HALO + d].astype(F32), axis=0, keepdims=True)
        for d in range(HALO)
    ]


def call(kernel, name, outs, specs, args, scratch=(), flops=2**20):
    return pl.pallas_call(
        kernel,
        out_shape=outs,
        in_specs=specs,
        out_specs=jax.tree.map(lambda _: VMEM, outs),
        scratch_shapes=scratch,
        compiler_params=pltpu.CompilerParams(vmem_limit_bytes=LIMIT),
        cost_estimate=pl.CostEstimate(flops=flops, bytes_accessed=2**20, transcendentals=0),
        name=name,
    )(*args)


def shape(*dims, dtype=BF16):
    return jax.ShapeDtypeStruct(dims, dtype)


def shift_kernel(q_row, mask, green, *rest):
    onehot, shifted = rest[-2:]
    kd, rounds = q_row.shape
    width = mask.shape[1]
    goal = jnp.zeros((1, onehot.shape[1]), jnp.int32)
    lane = iota(goal.shape, 1)
    for p in range(rounds * kd):
        goal = jnp.where(lane // HALO == p, q_row[p % kd, p // kd] * HALO + lane % HALO, goal)
    onehot[...] = (iota(onehot.shape, 0) == goal).astype(F32).astype(BF16)

    row, col = iota((width, width), 0), iota((width, width), 1)
    weights = jnp.broadcast_to(mask[...], (width, width)).astype(F32)
    for d in range(1, HALO + 1):
        move = jnp.where(col == row + d, weights, 0.0).astype(BF16)
        for k in range(kd):
            shifted[k * HALO + d - 1] = dot(move, green[0, k]).astype(BF16)


def halo_kernel(order, place, green, shifted, from_core, from_chip, full, first, extended):
    kd, width = green.shape[1:3]
    first_core = jnp.broadcast_to(place[1], from_core.shape) == 0
    core, chip = from_core[...].astype(F32), from_chip[...].astype(F32)
    before = jnp.where(first_core, chip, core).astype(BF16)
    after = jnp.where(first_core, core, chip).astype(BF16)
    rows, cols = iota((16, 16), 0), iota((16, 16), 1)
    row, col = iota((16, 64), 0), iota((16, 64), 1)
    kind = row // HALO
    pick = (col == kind * 16 + (1 - kind % 2) * (16 - HALO) + row % HALO).astype(F32).astype(BF16)
    for k in range(kd):
        for d in range(1, HALO + 1):
            at = k * HALO + d - 1
            wrap = (cols + 16 == rows + d).astype(F32).astype(BF16)
            moved = dot(wrap, after[2 * kd + k])
            full[at, : width - 16] = shifted[at, : width - 16]
            full[at, width - 16 :] = (shifted[at, width - 16 :].astype(F32) + moved).astype(BF16)
        ends = [before[k], after[k], before[kd + k], after[kd + k]]
        extended[k, :width] = green[0, k]
        extended[k, width:] = dot(pick, jnp.concatenate(ends, axis=0)).astype(BF16)
    lines = []
    for k in range(kd):
        lines += pair_products(green[1, order[k, 0]], full, k)
    first[...] = jnp.concatenate(lines, axis=0)


def terms_kernel(order, far, near, next_near, shifted, first, onehot, out):
    lines = [first[...]]
    for r, ref in ((1, far), (2, near), (3, next_near)):
        for k in range(far.shape[0]):
            lines += pair_products(ref[order[k, r]], shifted, k)
    terms = jnp.concatenate(lines, axis=0).astype(BF16)
    out[...] = dot(onehot[...], terms).astype(BF16)


def column_kernel(got, out):
    total = jnp.sum(got[...].astype(F32), axis=0).astype(BF16)
    half = out.shape[1]
    for dest in range(out.shape[0]):
        at = (dest // (out.shape[0] // 2)) * half
        out[dest] = total[at : at + half]


def weights_kernel(q_row, place, offsets, occupancy, coupling, mask, main, owner, *, scale):
    kd, rounds = q_row.shape
    width = mask.shape[1]
    modes = coupling.shape[0]
    pairs = rounds * kd

    q_col = jnp.zeros((pairs, coupling.shape[1]), jnp.int32)
    for p in range(pairs):
        q_col = jnp.where(iota(q_col.shape, 0) == p, q_row[p % kd, p // kd], q_col)
    chosen = (q_col == iota(q_col.shape, 1)).astype(F32)
    strength = lax.dot_general(
        chosen, coupling[...], (((1,), (1,)), ((), ())), precision=HIGHEST, preferred_element_type=F32
    )
    off_col = jnp.zeros((modes, width), jnp.int32)
    occ_col = jnp.zeros((modes, width), F32)
    for m in range(modes):
        off_col = jnp.where(iota(off_col.shape, 0) == m, offsets[m], off_col)
        occ_col = jnp.where(iota(off_col.shape, 0) == m, occupancy[m], occ_col)
    emit, absorb = [], []
    for d in range(1, HALO + 1):
        emit.append(dot(strength, jnp.where(off_col == d, occ_col + 1.0, 0.0), HIGHEST))
        absorb.append(dot(strength, jnp.where(off_col == d, occ_col, 0.0), HIGHEST))

    rows, cols = iota(owner.shape, 0), iota(owner.shape, 1)
    wide = (owner.shape[0], coupling.shape[1])
    mine = (iota(wide, 1) == place[0] + iota(wide, 0) // modes).astype(F32)
    factor = lax.dot_general(
        mine, coupling[...], (((1,), (1,)), ((), ())), precision=HIGHEST, preferred_element_type=F32
    )
    branch = iota(factor.shape, 1) == iota(factor.shape, 0) % modes
    factor = jnp.sum(jnp.where(branch, factor, 0.0), axis=1, keepdims=True) * scale
    off = jnp.zeros(owner.shape, jnp.int32)
    for m in range(modes):
        off = jnp.where(rows % modes == m, offsets[m], off)
    hit = (rows // modes == cols // HALO) & (off == cols % HALO + 1)
    owner[...] = jnp.where(hit, factor, 0.0)

    row, col = iota((width, width), 0), iota((width, width), 1)
    active = jnp.sum(jnp.where(row == col, mask[...], 0).astype(F32), axis=1, keepdims=True)
    live = jnp.where(active > 0.0, col - row, 2 * width)
    beyond = iota((width, 16), 1)
    source = jnp.where(beyond % 8 < HALO, beyond % 8 - HALO, width + beyond % 8 - HALO)
    gap = jnp.where(active > 0.0, source - iota((width, 16), 0), 2 * width)
    for comp in range(2):
        dif = jnp.where(beyond // 8 == comp, gap, 2 * width)
        for k in range(kd):
            ck = comp * kd + k
            ends = []
            for r in range(rounds):
                p = r * kd + k
                up = [x[p : p + 1, :] for x in emit]
                down = [x[p : p + 1, :] for x in absorb]
                if comp == 1:
                    up, down = down, up
                main[ck, :, r * width : (r + 1) * width] = band(live, up, down).astype(BF16)
                ends.append(band(dif, [x[:, :16] for x in up], [x[:, :16] for x in down]))
            main[ck, :, rounds * width :] = jnp.concatenate(ends, axis=1).astype(BF16)


def sigma_kernel(order, main, green, own, less1, less2, less3, great1, great2, great3, sigma):
    kd, rounds = order.shape
    width = green.shape[2]
    less = (own, less1, less2, less3)
    for k in range(kd):
        index = [order[k, r] for r in range(rounds)]
        ends = jnp.concatenate([x[i, width:] for x, i in zip(less, index)], axis=0)
        for comp in range(2):
            if comp == 0:
                blocks = [x[i, :width] for x, i in zip(less, index)]
            else:
                blocks = [green[1, index[0]]]
                blocks += [x[i] for x, i in zip((great1, great2, great3), index[1:])]
            weights = main[comp * kd + k]
            acc = dot(weights[:, : rounds * width], jnp.concatenate(blocks, axis=0))
            sigma[comp, k] = (acc + dot(weights[:, rounds * width :], ends)).astype(BF16)


def owner_kernel(got, owner, pol):
    total = jnp.sum(got[...].astype(F32), axis=0)
    pol[...] = dot(owner[...], total, HIGHEST)


def tie(x, y):
    return lax.optimization_barrier((x, y))[0]


def on_device(green, mask, pair_order, q_index, offsets, occupancy, coupling):
    _, kd, width, norb = green.shape
    rounds = pair_order.shape[0]
    count = lax.axis_size(("zl", "c"))
    owned = coupling.shape[0] // lax.axis_size(("x", "y", "zh"))
    order, q_row, spread, mask_row = pair_order[:, 0].T, q_index.T, coupling.T, mask[None, :]
    place = [lax.axis_index(("x", "y", "zh")) * owned, lax.axis_index("c")]
    place = jnp.stack([jnp.asarray(x, jnp.int32) for x in place])

    swap = [(0, 1), (1, 0)]

    def exchange(x):
        near = lax.ppermute(x, "y", [(i, i ^ 1) for i in range(4)])
        return near, lax.ppermute(x, "y", [(i, i ^ 2) for i in range(4)])

    more = green.reshape(-1, norb)[kd * width - 16 :]
    far = lax.ppermute(more, "zh", swap)[16:].reshape(kd, width, norb)
    first, last = green[:, :, :16], green[:, :, width - 16 :]
    masked = first[0] * mask[None, :16, None].astype(BF16)
    first_core = lax.axis_index("c") == 0

    def edge(x):
        return jnp.concatenate([x.reshape(2 * kd, 16, norb), masked], axis=0)

    from_core = lax.ppermute(edge(jnp.where(first_core, last, first)), "c", swap)
    meet = [(i, i + 1) for i in range(1, count - 1, 2)]
    to_chip = edge(jnp.where(first_core, first, last))
    from_chip = lax.ppermute(to_chip, ("zl", "c"), meet + [(j, i) for i, j in meet])
    great = (far, *exchange(tie(green[1], to_chip)))
    onehot, shifted = call(
        shift_kernel,
        "shift",
        (
            shape(coupling.shape[0] * HALO, rounds * kd * HALO),
            shape(kd * HALO, width, norb),
        ),
        [SMEM] + [VMEM] * 6,
        (q_row, mask_row, green, order, offsets[None], occupancy[None], spread),
    )
    shifted, first, extended = call(
        halo_kernel,
        "halo",
        (
            shape(*shifted.shape),
            shape(kd * HALO, norb, dtype=F32),
            shape(kd, width + 16, norb),
        ),
        [SMEM] * 2 + [VMEM] * 4,
        (order, place, green, shifted, from_core, from_chip),
    )
    dense = call(
        terms_kernel,
        "terms",
        shape(onehot.shape[0], norb),
        [SMEM] + [VMEM] * 6,
        (order, *great, shifted, first, onehot),
    )
    less = (lax.ppermute(extended, "zh", swap), *exchange(tie(extended, dense)))
    got = lax.all_to_all(dense.reshape(16, -1, norb), ("x", "y"), 0, 0, tiled=True)
    sent = call(
        column_kernel, "column", shape(2 * count, owned * HALO, norb), [VMEM], (got,)
    )
    got = lax.all_to_all(sent, ("zh", "zl", "c"), 0, 0, tiled=True)

    main, owner = call(
        functools.partial(weights_kernel, scale=1.0 / (width * count)),
        "weights",
        (
            shape(2 * kd, width, rounds * (width + 16)),
            shape(owned * offsets.shape[0], owned * HALO, dtype=F32),
        ),
        [SMEM] * 4 + [VMEM] * 2,
        (q_row, place, offsets, occupancy, tie(spread, sent), mask_row),
    )
    sigma = call(
        sigma_kernel,
        "sigma",
        shape(*green.shape),
        [SMEM] + [VMEM] * 9,
        (order, main, green, extended, *less, *great),
        flops=2**34,
    )
    pol = call(
        owner_kernel,
        "owner",
        shape(owner.shape[0], norb, dtype=F32),
        [VMEM] * 2,
        (got, owner),
    )
    return sigma, pol.reshape(owned, -1, norb)


def solution(mesh):
    split = Mesh(mesh.devices.reshape(4, 4, 2, 4, 2), AXES)
    mom, en = ("x", "y", "zh"), ("zl", "c")
    in_specs = (P(None, mom, en, None), P(en), P(None, mom, None), P(None, mom), P(), P(), P())
    out_specs = (P(None, mom, en, None), P(mom, None, None))
    return jax.shard_map(
        on_device, mesh=split, in_specs=in_specs, out_specs=out_specs, check_vma=False
    )
```

```python
import functools

import jax
import jax.numpy as jnp
from jax import lax
from jax.experimental import pallas as pl
from jax.experimental.pallas import tpu as pltpu
from jax.sharding import Mesh, PartitionSpec as P

HALO = 4
AXES = ("x", "y", "zh", "zl", "c")
F32 = jnp.float32
PIECES = 4
BF16 = jnp.bfloat16
HIGHEST = lax.Precision.HIGHEST
SMEM = pl.BlockSpec(memory_space=pltpu.SMEM)
LIMIT = 12 * 1024 * 1024
BEGIN_LIMIT = 12 * 1024 * 1024
VMEM = pl.BlockSpec(memory_space=pltpu.VMEM)


def iota(shape, dim):
    return lax.broadcasted_iota(jnp.int32, shape, dim)


def dot(a, b, precision=None):
    return lax.dot_general(
        a, b, (((1,), (0,)), ((), ())), precision=precision, preferred_element_type=F32
    )


def band(dif, above, below):
    out = jnp.zeros(dif.shape, F32)
    for d in range(1, HALO + 1):
        out = jnp.where(dif == d, above[d - 1], out)
        out = jnp.where(dif == -d, below[d - 1], out)
    return out


def pair_products(great, shifted, k):
    return [
        jnp.sum(great * shifted[k * HALO + d].astype(F32), axis=0, keepdims=True)
        for d in range(HALO)
    ]


def entry(table, i, j):
    return table[i : i + 1, j : j + 1]


def choose(blocks, index):
    low, high = blocks[0].astype(F32), blocks[1].astype(F32)
    return jnp.where(jnp.broadcast_to(index, low.shape) == 0, low, high)


def call(kernel, name, outs, specs, args, scratch=(), flops=2**20, out_specs=None):
    return pl.pallas_call(
        kernel,
        out_shape=outs,
        in_specs=specs,
        out_specs=out_specs or jax.tree.map(lambda _: VMEM, outs),
        scratch_shapes=scratch,
        compiler_params=pltpu.CompilerParams(vmem_limit_bytes=LIMIT),
        cost_estimate=pl.CostEstimate(flops=flops, bytes_accessed=2**20, transcendentals=0),
        name=name,
    )(*args)


def shape(*dims, dtype=BF16):
    return jax.ShapeDtypeStruct(dims, dtype)


def begin_kernel(green, *refs):
    count = (len(refs) - 3) // 2
    small, great, wide, kept, sems = refs[:count], refs[count], refs[count + 1], refs[count + 2 : -1], refs[-1]
    pairs = list(zip(small, kept))
    kd, width, _ = great.shape
    pairs.append((green.at[0, 0, pl.ds(0, 16)], wide.at[pl.ds(0, 16)]))
    for k in range(kd):
        pairs.append((green.at[1, k], great.at[k]))
        pairs.append((green.at[1, k], wide.at[pl.ds(16 + k * width, width)]))
    copies = [pltpu.make_async_copy(a, b, sems.at[i]) for i, (a, b) in enumerate(pairs)]
    for copy in reversed(copies):
        copy.start()
    for copy in copies:
        copy.wait()


def begin(green, *small):
    anywhere = pl.BlockSpec(memory_space=pltpu.HBM)
    _, kd, width, norb = green.shape
    outs = [shape(kd, width, norb), shape(16 + kd * width, norb)] + [shape(*x.shape, dtype=x.dtype) for x in small]
    green, *small = [pltpu.with_memory_space_constraint(x, pltpu.HBM) for x in (green, *small)]
    return pl.pallas_call(
        begin_kernel,
        out_shape=outs,
        in_specs=[anywhere] * (1 + len(small)),
        out_specs=[VMEM] * len(outs),
        scratch_shapes=[pltpu.SemaphoreType.DMA((len(small) + 2 * kd + 1,))],
        compiler_params=pltpu.CompilerParams(vmem_limit_bytes=BEGIN_LIMIT),
        cost_estimate=pl.CostEstimate(flops=0, bytes_accessed=2**18, transcendentals=0),
        name="begin",
    )(green, *small)


def shift_kernel(q_row, mask, green, onehot, shifted):
    kd, rounds = q_row.shape
    width = mask.shape[1]
    goal = jnp.zeros((1, onehot.shape[1]), jnp.int32)
    lane = iota(goal.shape, 1)
    for p in range(rounds * kd):
        goal = jnp.where(lane // HALO == p, entry(q_row, p % kd, p // kd) * HALO + lane % HALO, goal)
    onehot[...] = (iota(onehot.shape, 0) == goal).astype(F32).astype(BF16)

    row, col = iota((width, width), 0), iota((width, width), 1)
    weights = jnp.broadcast_to(mask[...], (width, width)).astype(F32)
    for d in range(1, HALO + 1):
        move = jnp.where(col == row + d, weights, 0.0).astype(BF16)
        for k in range(kd):
            shifted[k * HALO + d - 1] = dot(move, green[0, k]).astype(BF16)


def halo_kernel(order, place, green, shifted, from_core, from_chip, full, first, extended):
    kd, width = green.shape[1:3]
    first_core = jnp.broadcast_to(entry(place, 0, 1)[None], from_core.shape) == 0
    core, chip = from_core[...].astype(F32), from_chip[...].astype(F32)
    before = jnp.where(first_core, chip, core).astype(BF16)
    after = jnp.where(first_core, core, chip).astype(BF16)
    rows, cols = iota((16, 16), 0), iota((16, 16), 1)
    row, col = iota((16, 64), 0), iota((16, 64), 1)
    kind = row // HALO
    pick = (col == kind * 16 + (1 - kind % 2) * (16 - HALO) + row % HALO).astype(F32).astype(BF16)
    for k in range(kd):
        for d in range(1, HALO + 1):
            at = k * HALO + d - 1
            wrap = (cols + 16 == rows + d).astype(F32).astype(BF16)
            moved = dot(wrap, after[2 * kd + k])
            full[at, : width - 16] = shifted[at, : width - 16]
            full[at, width - 16 :] = (shifted[at, width - 16 :].astype(F32) + moved).astype(BF16)
        ends = [before[k], after[k], before[kd + k], after[kd + k]]
        extended[k, :width] = green[0, k]
        extended[k, width:] = dot(pick, jnp.concatenate(ends, axis=0)).astype(BF16)
    lines = []
    for k in range(kd):
        lines += pair_products(choose(green[1], entry(order, k, 0)), full, k)
    first[...] = jnp.concatenate(lines, axis=0)


def terms_kernel(order, far, near, next_near, shifted, first, onehot, out, held, sems):
    lines = [first[...]]
    for r, ref in ((1, far), (2, near), (3, next_near)):
        for k in range(far.shape[0]):
            lines += pair_products(choose(ref, entry(order, k, r)), shifted, k)
    terms = jnp.concatenate(lines, axis=0).astype(BF16)
    step = out.shape[0] // PIECES
    copies = []
    for i in range(PIECES):
        rows = pl.ds(i * step, step)
        held[rows] = dot(onehot[rows], terms).astype(BF16)
        copies.append(pltpu.make_async_copy(held.at[rows], out.at[rows], sems.at[i]))
        copies[-1].start()
    for copy in copies:
        copy.wait()


def column_kernel(got, out):
    total = jnp.sum(got[...].astype(F32), axis=0).astype(BF16)
    half = out.shape[1]
    for dest in range(out.shape[0]):
        at = (dest // (out.shape[0] // 2)) * half
        out[dest] = total[at : at + half]


def weights_kernel(q_row, place, offsets, occupancy, coupling, mask, main, owner, *, scale):
    kd, rounds = q_row.shape
    width = mask.shape[1]
    modes = coupling.shape[0]
    pairs = rounds * kd

    q_col = jnp.zeros((pairs, coupling.shape[1]), jnp.int32)
    for p in range(pairs):
        q_col = jnp.where(iota(q_col.shape, 0) == p, q_row[p % kd, p // kd], q_col)
    chosen = (q_col == iota(q_col.shape, 1)).astype(F32)
    strength = lax.dot_general(
        chosen, coupling[...], (((1,), (1,)), ((), ())), precision=HIGHEST, preferred_element_type=F32
    )
    off_col = jnp.zeros((modes, width), jnp.int32)
    occ_col = jnp.zeros((modes, width), F32)
    for m in range(modes):
        off_col = jnp.where(iota(off_col.shape, 0) == m, offsets[0, m], off_col)
        occ_col = jnp.where(iota(off_col.shape, 0) == m, occupancy[0, m], occ_col)
    emit, absorb = [], []
    for d in range(1, HALO + 1):
        emit.append(dot(strength, jnp.where(off_col == d, occ_col + 1.0, 0.0), HIGHEST))
        absorb.append(dot(strength, jnp.where(off_col == d, occ_col, 0.0), HIGHEST))

    rows, cols = iota(owner.shape, 0), iota(owner.shape, 1)
    wide = (owner.shape[0], coupling.shape[1])
    mine = (iota(wide, 1) == place[0, 0] + iota(wide, 0) // modes).astype(F32)
    factor = lax.dot_general(
        mine, coupling[...], (((1,), (1,)), ((), ())), precision=HIGHEST, preferred_element_type=F32
    )
    branch = iota(factor.shape, 1) == iota(factor.shape, 0) % modes
    factor = jnp.sum(jnp.where(branch, factor, 0.0), axis=1, keepdims=True) * scale
    off = jnp.zeros(owner.shape, jnp.int32)
    for m in range(modes):
        off = jnp.where(rows % modes == m, offsets[0, m], off)
    hit = (rows // modes == cols // HALO) & (off == cols % HALO + 1)
    owner[...] = jnp.where(hit, factor, 0.0)

    row, col = iota((width, width), 0), iota((width, width), 1)
    active = jnp.sum(jnp.where(row == col, mask[...], 0).astype(F32), axis=1, keepdims=True)
    live = jnp.where(active > 0.0, col - row, 2 * width)
    beyond = iota((width, 16), 1)
    source = jnp.where(beyond % 8 < HALO, beyond % 8 - HALO, width + beyond % 8 - HALO)
    gap = jnp.where(active > 0.0, source - iota((width, 16), 0), 2 * width)
    for comp in range(2):
        dif = jnp.where(beyond // 8 == comp, gap, 2 * width)
        for k in range(kd):
            ck = comp * kd + k
            ends = []
            for r in range(rounds):
                p = r * kd + k
                up = [x[p : p + 1, :] for x in emit]
                down = [x[p : p + 1, :] for x in absorb]
                if comp == 1:
                    up, down = down, up
                main[ck, :, r * width : (r + 1) * width] = band(live, up, down).astype(BF16)
                ends.append(band(dif, [x[:, :16] for x in up], [x[:, :16] for x in down]))
            main[ck, :, rounds * width :] = jnp.concatenate(ends, axis=1).astype(BF16)


def sigma_kernel(order, main, green, own, less1, less2, less3, great1, great2, great3, sigma):
    kd, rounds = order.shape
    width = green.shape[2]
    less = (own, less1, less2, less3)
    for k in range(kd):
        index = [order[k, r] for r in range(rounds)]
        ends = jnp.concatenate([x[i, width:] for x, i in zip(less, index)], axis=0)
        for comp in range(2):
            if comp == 0:
                blocks = [x[i, :width] for x, i in zip(less, index)]
            else:
                blocks = [green[1, index[0]]]
                blocks += [x[i] for x, i in zip((great1, great2, great3), index[1:])]
            weights = main[comp * kd + k]
            acc = dot(weights[:, : rounds * width], jnp.concatenate(blocks, axis=0))
            sigma[comp, k] = (acc + dot(weights[:, rounds * width :], ends)).astype(BF16)


def owner_kernel(got, owner, pol):
    total = jnp.sum(got[...].astype(F32), axis=0)
    pol[...] = dot(owner[...], total, HIGHEST)


def tie(x, y):
    return lax.optimization_barrier((x, y))[0]


def on_device(green, mask, pair_order, q_index, offsets, occupancy, coupling):
    _, kd, width, norb = green.shape
    rounds = pair_order.shape[0]
    count = lax.axis_size(("zl", "c"))
    owned = coupling.shape[0] // lax.axis_size(("x", "y", "zh"))
    mine, wide, order, q_row, spread, mask_row, offset_row, occupancy_row = begin(
        green,
        pair_order[:, 0].T,
        q_index.T,
        coupling.T,
        mask[None, :],
        offsets[None, :],
        occupancy[None, :],
    )
    place = [lax.axis_index(("x", "y", "zh")) * owned, lax.axis_index("c")]
    place = jnp.stack([jnp.asarray(x, jnp.int32) for x in place])[None]

    swap = [(0, 1), (1, 0)]

    def exchange(x):
        near = lax.ppermute(x, "y", [(i, i ^ 1) for i in range(4)])
        return near, lax.ppermute(x, "y", [(i, i ^ 2) for i in range(4)])

    far = lax.ppermute(wide, "zh", swap)[16:].reshape(kd, width, norb)
    first, last = green[:, :, :16], green[:, :, width - 16 :]
    masked = first[0] * mask_row[0, None, :16, None].astype(BF16)
    first_core = lax.axis_index("c") == 0

    def edge(x):
        return jnp.concatenate([x.reshape(2 * kd, 16, norb), masked], axis=0)

    from_core = lax.ppermute(edge(jnp.where(first_core, last, first)), "c", swap)
    meet = [(i, i + 1) for i in range(1, count - 1, 2)]
    to_chip = edge(jnp.where(first_core, first, last))
    from_chip = lax.ppermute(to_chip, ("zl", "c"), meet + [(j, i) for i, j in meet])
    great = (far, *exchange(tie(mine, to_chip)))
    onehot, shifted = call(
        shift_kernel,
        "shift",
        (
            shape(coupling.shape[0] * HALO, rounds * kd * HALO),
            shape(kd * HALO, width, norb),
        ),
        [VMEM] * 3,
        (q_row, mask_row, green),
    )
    shifted, first, extended = call(
        halo_kernel,
        "halo",
        (
            shape(*shifted.shape),
            shape(kd * HALO, norb, dtype=F32),
            shape(kd, width + 16, norb),
        ),
        [VMEM] * 6,
        (order, place, green, shifted, from_core, from_chip),
    )
    dense = call(
        terms_kernel,
        "terms",
        shape(onehot.shape[0], norb),
        [VMEM] * 7,
        (order, *great, shifted, first, onehot),
        scratch=[pltpu.VMEM((onehot.shape[0], norb), BF16), pltpu.SemaphoreType.DMA((PIECES,))],
        out_specs=pl.BlockSpec(memory_space=pl.ANY),
    )
    less = (lax.ppermute(extended, "zh", swap), *exchange(tie(extended, dense)))
    got = lax.all_to_all(dense.reshape(16, -1, norb), ("x", "y"), 0, 0, tiled=True)
    sent = call(
        column_kernel, "column", shape(2 * count, owned * HALO, norb), [VMEM], (got,)
    )
    got = lax.all_to_all(sent, ("zh", "zl", "c"), 0, 0, tiled=True)

    main, owner = call(
        functools.partial(weights_kernel, scale=1.0 / (width * count)),
        "weights",
        (
            shape(2 * kd, width, rounds * (width + 16)),
            shape(owned * offsets.shape[0], owned * HALO, dtype=F32),
        ),
        [SMEM] * 4 + [VMEM] * 2,
        (q_row, place, offset_row, occupancy_row, tie(spread, sent), mask_row),
    )
    sigma = call(
        sigma_kernel,
        "sigma",
        shape(*green.shape),
        [SMEM] + [VMEM] * 9,
        (order, main, green, extended, *less, *great),
        flops=2**34,
    )
    pol = call(
        owner_kernel,
        "owner",
        shape(owner.shape[0], norb, dtype=F32),
        [VMEM] * 2,
        (got, owner),
    )
    return sigma, pol.reshape(owned, -1, norb)


def solution(mesh):
    split = Mesh(mesh.devices.reshape(4, 4, 2, 4, 2), AXES)
    mom, en = ("x", "y", "zh"), ("zl", "c")
    in_specs = (P(None, mom, en, None), P(en), P(None, mom, None), P(None, mom), P(), P(), P())
    out_specs = (P(None, mom, en, None), P(mom, None, None))
    return jax.shard_map(
        on_device, mesh=split, in_specs=in_specs, out_specs=out_specs, check_vma=False
    )
```

```python
import functools

import jax
import jax.numpy as jnp
from jax import lax
from jax.experimental import pallas as pl
from jax.experimental.pallas import tpu as pltpu
from jax.sharding import Mesh, PartitionSpec as P

HALO = 4
AXES = ("x", "y", "zh", "zl", "c")
F32 = jnp.float32
PIECES = 4
BF16 = jnp.bfloat16
HIGHEST = lax.Precision.HIGHEST
SMEM = pl.BlockSpec(memory_space=pltpu.SMEM)
LIMIT = 12 * 1024 * 1024
BEGIN_LIMIT = 12 * 1024 * 1024
VMEM = pl.BlockSpec(memory_space=pltpu.VMEM)


def iota(shape, dim):
    return lax.broadcasted_iota(jnp.int32, shape, dim)


def dot(a, b, precision=None):
    return lax.dot_general(
        a, b, (((1,), (0,)), ((), ())), precision=precision, preferred_element_type=F32
    )


def band(dif, above, below):
    out = jnp.zeros(dif.shape, F32)
    for d in range(1, HALO + 1):
        out = jnp.where(dif == d, above[d - 1], out)
        out = jnp.where(dif == -d, below[d - 1], out)
    return out


def pair_products(great, shifted, k):
    return [
        jnp.sum(great * shifted[k * HALO + d].astype(F32), axis=0, keepdims=True)
        for d in range(HALO)
    ]


def entry(table, i, j):
    return table[i : i + 1, j : j + 1]


def choose(blocks, index):
    low, high = blocks[0].astype(F32), blocks[1].astype(F32)
    return jnp.where(jnp.broadcast_to(index, low.shape) == 0, low, high)


def call(kernel, name, outs, specs, args, scratch=(), flops=2**20, out_specs=None):
    return pl.pallas_call(
        kernel,
        out_shape=outs,
        in_specs=specs,
        out_specs=out_specs or jax.tree.map(lambda _: VMEM, outs),
        scratch_shapes=scratch,
        compiler_params=pltpu.CompilerParams(vmem_limit_bytes=LIMIT),
        cost_estimate=pl.CostEstimate(flops=flops, bytes_accessed=2**20, transcendentals=0),
        name=name,
    )(*args)


def shape(*dims, dtype=BF16):
    return jax.ShapeDtypeStruct(dims, dtype)


def begin_kernel(green, *refs):
    count = (len(refs) - 3) // 2
    small, great, wide, kept, sems = refs[:count], refs[count], refs[count + 1], refs[count + 2 : -1], refs[-1]
    pairs = list(zip(small, kept))
    kd, width, _ = great.shape
    pairs.append((green.at[0, 0, pl.ds(0, 16)], wide.at[pl.ds(0, 16)]))
    for k in range(kd):
        pairs.append((green.at[1, k], great.at[k]))
        pairs.append((green.at[1, k], wide.at[pl.ds(16 + k * width, width)]))
    copies = [pltpu.make_async_copy(a, b, sems.at[i]) for i, (a, b) in enumerate(pairs)]
    for copy in reversed(copies):
        copy.start()
    for copy in copies:
        copy.wait()


def begin(green, *small):
    anywhere = pl.BlockSpec(memory_space=pltpu.HBM)
    _, kd, width, norb = green.shape
    outs = [shape(kd, width, norb), shape(16 + kd * width, norb)] + [shape(*x.shape, dtype=x.dtype) for x in small]
    green, *small = [pltpu.with_memory_space_constraint(x, pltpu.HBM) for x in (green, *small)]
    return pl.pallas_call(
        begin_kernel,
        out_shape=outs,
        in_specs=[anywhere] * (1 + len(small)),
        out_specs=[VMEM] * len(outs),
        scratch_shapes=[pltpu.SemaphoreType.DMA((len(small) + 2 * kd + 1,))],
        compiler_params=pltpu.CompilerParams(vmem_limit_bytes=BEGIN_LIMIT),
        cost_estimate=pl.CostEstimate(flops=0, bytes_accessed=2**18, transcendentals=0),
        name="begin",
    )(green, *small)


def shift_kernel(q_row, mask, green, onehot, shifted):
    kd, rounds = q_row.shape
    width = mask.shape[1]
    goal = jnp.zeros((1, onehot.shape[1]), jnp.int32)
    lane = iota(goal.shape, 1)
    for p in range(rounds * kd):
        goal = jnp.where(lane // HALO == p, entry(q_row, p % kd, p // kd) * HALO + lane % HALO, goal)
    onehot[...] = (iota(onehot.shape, 0) == goal).astype(F32).astype(BF16)

    row, col = iota((width, width), 0), iota((width, width), 1)
    weights = jnp.broadcast_to(mask[...], (width, width)).astype(F32)
    for d in range(1, HALO + 1):
        move = jnp.where(col == row + d, weights, 0.0).astype(BF16)
        for k in range(kd):
            shifted[k * HALO + d - 1] = dot(move, green[0, k]).astype(BF16)


def halo_kernel(order, place, green, shifted, from_core, from_chip, full, first, extended):
    kd, width = green.shape[1:3]
    first_core = jnp.broadcast_to(entry(place, 0, 1)[None], from_core.shape) == 0
    core, chip = from_core[...].astype(F32), from_chip[...].astype(F32)
    before = jnp.where(first_core, chip, core).astype(BF16)
    after = jnp.where(first_core, core, chip).astype(BF16)
    rows, cols = iota((16, 16), 0), iota((16, 16), 1)
    row, col = iota((16, 64), 0), iota((16, 64), 1)
    kind = row // HALO
    pick = (col == kind * 16 + (1 - kind % 2) * (16 - HALO) + row % HALO).astype(F32).astype(BF16)
    for k in range(kd):
        for d in range(1, HALO + 1):
            at = k * HALO + d - 1
            wrap = (cols + 16 == rows + d).astype(F32).astype(BF16)
            moved = dot(wrap, after[2 * kd + k])
            full[at, : width - 16] = shifted[at, : width - 16]
            full[at, width - 16 :] = (shifted[at, width - 16 :].astype(F32) + moved).astype(BF16)
        ends = [before[k], after[k], before[kd + k], after[kd + k]]
        extended[k, :width] = green[0, k]
        extended[k, width:] = dot(pick, jnp.concatenate(ends, axis=0)).astype(BF16)
    lines = []
    for k in range(kd):
        lines += pair_products(choose(green[1], entry(order, k, 0)), full, k)
    first[...] = jnp.concatenate(lines, axis=0)


def terms_kernel(order, far, near, next_near, shifted, first, onehot, out, held, sems):
    lines = [first[...]]
    for r, ref in ((1, far), (2, near), (3, next_near)):
        for k in range(far.shape[0]):
            lines += pair_products(choose(ref, entry(order, k, r)), shifted, k)
    terms = jnp.concatenate(lines, axis=0).astype(BF16)
    step = out.shape[0] // PIECES
    copies = []
    for i in range(PIECES):
        rows = pl.ds(i * step, step)
        held[rows] = dot(onehot[rows], terms).astype(BF16)
        copies.append(pltpu.make_async_copy(held.at[rows], out.at[rows], sems.at[i]))
        copies[-1].start()
    for copy in copies:
        copy.wait()


def column_kernel(got, out):
    total = jnp.sum(got[...].astype(F32), axis=0).astype(BF16)
    half = out.shape[1]
    for dest in range(out.shape[0]):
        at = dest // (out.shape[0] // 4) % 2 * half
        out[dest] = total[at : at + half]


def weights_kernel(q_row, place, offsets, occupancy, coupling, mask, main, owner, *, scale):
    kd, rounds = q_row.shape
    width = mask.shape[1]
    modes = coupling.shape[0]
    pairs = rounds * kd

    q_col = jnp.zeros((pairs, coupling.shape[1]), jnp.int32)
    for p in range(pairs):
        q_col = jnp.where(iota(q_col.shape, 0) == p, q_row[p % kd, p // kd], q_col)
    chosen = (q_col == iota(q_col.shape, 1)).astype(F32)
    strength = lax.dot_general(
        chosen, coupling[...], (((1,), (1,)), ((), ())), precision=HIGHEST, preferred_element_type=F32
    )
    off_col = jnp.zeros((modes, width), jnp.int32)
    occ_col = jnp.zeros((modes, width), F32)
    for m in range(modes):
        off_col = jnp.where(iota(off_col.shape, 0) == m, offsets[0, m], off_col)
        occ_col = jnp.where(iota(off_col.shape, 0) == m, occupancy[0, m], occ_col)
    emit, absorb = [], []
    for d in range(1, HALO + 1):
        emit.append(dot(strength, jnp.where(off_col == d, occ_col + 1.0, 0.0), HIGHEST))
        absorb.append(dot(strength, jnp.where(off_col == d, occ_col, 0.0), HIGHEST))

    rows, cols = iota(owner.shape, 0), iota(owner.shape, 1)
    wide = (owner.shape[0], coupling.shape[1])
    mine = (iota(wide, 1) == place[0, 0] + iota(wide, 0) // modes).astype(F32)
    factor = lax.dot_general(
        mine, coupling[...], (((1,), (1,)), ((), ())), precision=HIGHEST, preferred_element_type=F32
    )
    branch = iota(factor.shape, 1) == iota(factor.shape, 0) % modes
    factor = jnp.sum(jnp.where(branch, factor, 0.0), axis=1, keepdims=True) * scale
    off = jnp.zeros(owner.shape, jnp.int32)
    for m in range(modes):
        off = jnp.where(rows % modes == m, offsets[0, m], off)
    hit = (rows // modes == cols // HALO) & (off == cols % HALO + 1)
    owner[...] = jnp.where(hit, factor, 0.0)

    row, col = iota((width, width), 0), iota((width, width), 1)
    active = jnp.sum(jnp.where(row == col, mask[...], 0).astype(F32), axis=1, keepdims=True)
    live = jnp.where(active > 0.0, col - row, 2 * width)
    beyond = iota((width, 16), 1)
    source = jnp.where(beyond % 8 < HALO, beyond % 8 - HALO, width + beyond % 8 - HALO)
    gap = jnp.where(active > 0.0, source - iota((width, 16), 0), 2 * width)
    for comp in range(2):
        dif = jnp.where(beyond // 8 == comp, gap, 2 * width)
        for k in range(kd):
            ck = comp * kd + k
            ends = []
            for r in range(rounds):
                p = r * kd + k
                up = [x[p : p + 1, :] for x in emit]
                down = [x[p : p + 1, :] for x in absorb]
                if comp == 1:
                    up, down = down, up
                main[ck, :, r * width : (r + 1) * width] = band(live, up, down).astype(BF16)
                ends.append(band(dif, [x[:, :16] for x in up], [x[:, :16] for x in down]))
            main[ck, :, rounds * width :] = jnp.concatenate(ends, axis=1).astype(BF16)


def sigma_kernel(order, main, green, own, less1, less2, less3, great1, great2, great3, sigma):
    kd, rounds = order.shape
    width = green.shape[2]
    less = (own, less1, less2, less3)
    for k in range(kd):
        index = [order[k, r] for r in range(rounds)]
        ends = jnp.concatenate([x[i, width:] for x, i in zip(less, index)], axis=0)
        for comp in range(2):
            if comp == 0:
                blocks = [x[i, :width] for x, i in zip(less, index)]
            else:
                blocks = [green[1, index[0]]]
                blocks += [x[i] for x, i in zip((great1, great2, great3), index[1:])]
            weights = main[comp * kd + k]
            acc = dot(weights[:, : rounds * width], jnp.concatenate(blocks, axis=0))
            sigma[comp, k] = (acc + dot(weights[:, rounds * width :], ends)).astype(BF16)


def owner_kernel(got, owner, pol):
    total = jnp.sum(got[...].astype(F32), axis=0)
    pol[...] = dot(owner[...], total, HIGHEST)


def tie(x, y):
    return lax.optimization_barrier((x, y))[0]


def on_device(green, mask, pair_order, q_index, offsets, occupancy, coupling):
    _, kd, width, norb = green.shape
    rounds = pair_order.shape[0]
    count = lax.axis_size(("zl", "c"))
    owned = coupling.shape[0] // lax.axis_size(("x", "y", "zh"))
    mine, wide, order, q_row, spread, mask_row, offset_row, occupancy_row = begin(
        green,
        pair_order[:, 0].T,
        q_index.T,
        coupling.T,
        mask[None, :],
        offsets[None, :],
        occupancy[None, :],
    )
    place = [lax.axis_index(("x", "y", "zh")) * owned, lax.axis_index("c")]
    place = jnp.stack([jnp.asarray(x, jnp.int32) for x in place])[None]

    swap = [(0, 1), (1, 0)]

    def exchange(x):
        near = lax.ppermute(x, "y", [(i, i ^ 1) for i in range(4)])
        return near, lax.ppermute(x, "y", [(i, i ^ 2) for i in range(4)])

    far = lax.ppermute(wide, "zh", swap)[16:].reshape(kd, width, norb)
    first, last = green[:, :, :16], green[:, :, width - 16 :]
    masked = first[0] * mask_row[0, None, :16, None].astype(BF16)
    first_core = lax.axis_index("c") == 0

    def edge(x):
        return jnp.concatenate([x.reshape(2 * kd, 16, norb), masked], axis=0)

    from_core = lax.ppermute(edge(jnp.where(first_core, last, first)), "c", swap)
    meet = [(i, i + 1) for i in range(1, count - 1, 2)]
    to_chip = edge(jnp.where(first_core, first, last))
    from_chip = lax.ppermute(to_chip, ("zl", "c"), meet + [(j, i) for i, j in meet])
    great = (far, *exchange(tie(mine, to_chip)))
    onehot, shifted = call(
        shift_kernel,
        "shift",
        (
            shape(coupling.shape[0] * HALO, rounds * kd * HALO),
            shape(kd * HALO, width, norb),
        ),
        [VMEM] * 3,
        (q_row, mask_row, green),
    )
    shifted, first, extended = call(
        halo_kernel,
        "halo",
        (
            shape(*shifted.shape),
            shape(kd * HALO, norb, dtype=F32),
            shape(kd, width + 16, norb),
        ),
        [VMEM] * 6,
        (order, place, green, shifted, from_core, from_chip),
    )
    dense = call(
        terms_kernel,
        "terms",
        shape(onehot.shape[0], norb),
        [VMEM] * 7,
        (order, *great, shifted, first, onehot),
        scratch=[pltpu.VMEM((onehot.shape[0], norb), BF16), pltpu.SemaphoreType.DMA((PIECES,))],
        out_specs=pl.BlockSpec(memory_space=pl.ANY),
    )
    less = (lax.ppermute(extended, "zh", swap), *exchange(tie(extended, dense)))
    got = lax.all_to_all(dense.reshape(16, -1, norb), ("x", "y"), 0, 0, tiled=True)
    sent = call(
        column_kernel, "column", shape(2 * count, owned * HALO, norb), [VMEM], (got,)
    )
    got = lax.all_to_all(sent, ("c", "zh", "zl"), 0, 0, tiled=True)

    main, owner = call(
        functools.partial(weights_kernel, scale=1.0 / (width * count)),
        "weights",
        (
            shape(2 * kd, width, rounds * (width + 16)),
            shape(owned * offsets.shape[0], owned * HALO, dtype=F32),
        ),
        [SMEM] * 4 + [VMEM] * 2,
        (q_row, place, offset_row, occupancy_row, tie(spread, sent), mask_row),
    )
    sigma = call(
        sigma_kernel,
        "sigma",
        shape(*green.shape),
        [SMEM] + [VMEM] * 9,
        (order, main, green, extended, *less, *great),
        flops=2**34,
    )
    pol = call(
        owner_kernel,
        "owner",
        shape(owner.shape[0], norb, dtype=F32),
        [VMEM] * 2,
        (got, owner),
    )
    return sigma, pol.reshape(owned, -1, norb)


def solution(mesh):
    split = Mesh(mesh.devices.reshape(4, 4, 2, 4, 2), AXES)
    mom, en = ("x", "y", "zh"), ("zl", "c")
    in_specs = (P(None, mom, en, None), P(en), P(None, mom, None), P(None, mom), P(), P(), P())
    out_specs = (P(None, mom, en, None), P(mom, None, None))
    return jax.shard_map(
        on_device, mesh=split, in_specs=in_specs, out_specs=out_specs, check_vma=False
    )
```

```python
import functools

import jax
import jax.numpy as jnp
from jax import lax
from jax.experimental import pallas as pl
from jax.experimental.pallas import tpu as pltpu
from jax.sharding import Mesh, PartitionSpec as P

HALO = 4
AXES = ("x", "y", "zh", "zl", "c")
F32 = jnp.float32
PIECES = 4
BF16 = jnp.bfloat16
HIGHEST = lax.Precision.HIGHEST
SMEM = pl.BlockSpec(memory_space=pltpu.SMEM)
LIMIT = 12 * 1024 * 1024
BEGIN_LIMIT = 12 * 1024 * 1024
VMEM = pl.BlockSpec(memory_space=pltpu.VMEM)


def iota(shape, dim):
    return lax.broadcasted_iota(jnp.int32, shape, dim)


def dot(a, b, precision=None):
    return lax.dot_general(
        a, b, (((1,), (0,)), ((), ())), precision=precision, preferred_element_type=F32
    )


def band(dif, above, below):
    out = jnp.zeros(dif.shape, F32)
    for d in range(1, HALO + 1):
        out = jnp.where(dif == d, above[d - 1], out)
        out = jnp.where(dif == -d, below[d - 1], out)
    return out


def pair_products(great, shifted, k):
    return [
        jnp.sum(great * shifted[k * HALO + d].astype(F32), axis=0, keepdims=True)
        for d in range(HALO)
    ]


def entry(table, i, j):
    return table[i : i + 1, j : j + 1]


def choose(blocks, index):
    low, high = blocks[0][...].astype(F32), blocks[1][...].astype(F32)
    return jnp.where(jnp.broadcast_to(index, low.shape) == 0, low, high)


def call(kernel, name, outs, specs, args, scratch=(), flops=2**20, out_specs=None):
    return pl.pallas_call(
        kernel,
        out_shape=outs,
        in_specs=specs,
        out_specs=out_specs or jax.tree.map(lambda _: VMEM, outs),
        scratch_shapes=scratch,
        compiler_params=pltpu.CompilerParams(vmem_limit_bytes=LIMIT),
        cost_estimate=pl.CostEstimate(flops=flops, bytes_accessed=2**20, transcendentals=0),
        name=name,
    )(*args)


def shape(*dims, dtype=BF16):
    return jax.ShapeDtypeStruct(dims, dtype)


def begin_kernel(green, *refs):
    count = (len(refs) - 2) // 2
    small, great, kept, sems = refs[:count], refs[count], refs[count + 1 : -1], refs[-1]
    pairs = list(zip(small, kept))
    for k in range(great.shape[0]):
        pairs.append((green.at[1, k], great.at[k]))
    copies = [pltpu.make_async_copy(a, b, sems.at[i]) for i, (a, b) in enumerate(pairs)]
    for copy in reversed(copies):
        copy.start()
    for copy in copies:
        copy.wait()


def begin(green, *small):
    anywhere = pl.BlockSpec(memory_space=pltpu.HBM)
    _, kd, width, norb = green.shape
    outs = [shape(kd, width, norb)] + [shape(*x.shape, dtype=x.dtype) for x in small]
    green, *small = [pltpu.with_memory_space_constraint(x, pltpu.HBM) for x in (green, *small)]
    return pl.pallas_call(
        begin_kernel,
        out_shape=outs,
        in_specs=[anywhere] * (1 + len(small)),
        out_specs=[VMEM] * len(outs),
        scratch_shapes=[pltpu.SemaphoreType.DMA((len(small) + kd,))],
        compiler_params=pltpu.CompilerParams(vmem_limit_bytes=BEGIN_LIMIT),
        cost_estimate=pl.CostEstimate(flops=0, bytes_accessed=2**18, transcendentals=0),
        name="begin",
    )(green, *small)


def shift_kernel(q_row, mask, green, onehot, shifted):
    kd, rounds = q_row.shape
    width = mask.shape[1]
    goal = jnp.zeros((1, onehot.shape[1]), jnp.int32)
    lane = iota(goal.shape, 1)
    for p in range(rounds * kd):
        goal = jnp.where(lane // HALO == p, entry(q_row, p % kd, p // kd) * HALO + lane % HALO, goal)
    onehot[...] = (iota(onehot.shape, 0) == goal).astype(F32).astype(BF16)

    row, col = iota((width, width), 0), iota((width, width), 1)
    weights = jnp.broadcast_to(mask[...], (width, width)).astype(F32)
    for d in range(1, HALO + 1):
        move = jnp.where(col == row + d, weights, 0.0).astype(BF16)
        for k in range(kd):
            shifted[k * HALO + d - 1] = dot(move, green[0, k]).astype(BF16)


def halo_kernel(order, place, green, shifted, from_core, from_chip, full, first, extended):
    kd, width = green.shape[1:3]
    first_core = jnp.broadcast_to(entry(place, 0, 1)[None], from_core.shape) == 0
    core, chip = from_core[...].astype(F32), from_chip[...].astype(F32)
    before = jnp.where(first_core, chip, core).astype(BF16)
    after = jnp.where(first_core, core, chip).astype(BF16)
    size = before.shape[0] * before.shape[1]
    before, after = before.reshape(size, -1), after.reshape(size, -1)
    both = jnp.concatenate([before, after], axis=0)
    rows, cols = iota((16, size), 0), iota((16, size), 1)
    row, col = iota((16, 2 * size), 0), iota((16, 2 * size), 1)
    kind = row // HALO
    source = kind // 2 * 8 * kd + kind % 2 * size + (1 - kind % 2) * (8 - HALO) + row % HALO
    for k in range(kd):
        for d in range(1, HALO + 1):
            at = k * HALO + d - 1
            wrap = (rows + d >= 16) & (cols == rows + d - 16 + (2 * kd + k) * 8)
            moved = dot(wrap.astype(F32).astype(BF16), after)
            full[at, : width - 16] = shifted[at, : width - 16]
            full[at, width - 16 :] = (shifted[at, width - 16 :].astype(F32) + moved).astype(BF16)
        extended[k, :width] = green[0, k]
        pick = (col == source + 8 * k).astype(F32).astype(BF16)
        extended[k, width:] = dot(pick, both).astype(BF16)
    lines = []
    for k in range(kd):
        lines += pair_products(choose(green.at[1], entry(order, k, 0)), full, k)
    first[...] = jnp.concatenate(lines, axis=0)


def terms_kernel(order, far0, far1, near, next_near, shifted, first, onehot, out, held, sems):
    lines = [first[...]]
    far = (far0, far1)
    for r, ref in ((1, far), (2, near), (3, next_near)):
        for k in range(len(far)):
            lines += pair_products(choose(ref, entry(order, k, r)), shifted, k)
    terms = jnp.concatenate(lines, axis=0).astype(BF16)
    step = out.shape[0] // PIECES
    copies = []
    for i in range(PIECES):
        rows = pl.ds(i * step, step)
        held[rows] = dot(onehot[rows], terms).astype(BF16)
        copies.append(pltpu.make_async_copy(held.at[rows], out.at[rows], sems.at[i]))
        copies[-1].start()
    for copy in copies:
        copy.wait()


def column_kernel(got, out):
    total = jnp.sum(got[...].astype(F32), axis=0).astype(BF16)
    half = out.shape[1]
    for dest in range(out.shape[0]):
        at = dest // (out.shape[0] // 4) % 2 * half
        out[dest] = total[at : at + half]


def weights_kernel(q_row, place, offsets, occupancy, coupling, mask, main, owner, *, scale):
    kd, rounds = q_row.shape
    width = mask.shape[1]
    modes = coupling.shape[0]
    pairs = rounds * kd

    q_col = jnp.zeros((pairs, coupling.shape[1]), jnp.int32)
    for p in range(pairs):
        q_col = jnp.where(iota(q_col.shape, 0) == p, q_row[p % kd, p // kd], q_col)
    chosen = (q_col == iota(q_col.shape, 1)).astype(F32)
    strength = lax.dot_general(
        chosen, coupling[...], (((1,), (1,)), ((), ())), precision=HIGHEST, preferred_element_type=F32
    )
    off_col = jnp.zeros((modes, width), jnp.int32)
    occ_col = jnp.zeros((modes, width), F32)
    for m in range(modes):
        off_col = jnp.where(iota(off_col.shape, 0) == m, offsets[0, m], off_col)
        occ_col = jnp.where(iota(off_col.shape, 0) == m, occupancy[0, m], occ_col)
    emit, absorb = [], []
    for d in range(1, HALO + 1):
        emit.append(dot(strength, jnp.where(off_col == d, occ_col + 1.0, 0.0), HIGHEST))
        absorb.append(dot(strength, jnp.where(off_col == d, occ_col, 0.0), HIGHEST))

    rows, cols = iota(owner.shape, 0), iota(owner.shape, 1)
    wide = (owner.shape[0], coupling.shape[1])
    mine = (iota(wide, 1) == place[0, 0] + iota(wide, 0) // modes).astype(F32)
    factor = lax.dot_general(
        mine, coupling[...], (((1,), (1,)), ((), ())), precision=HIGHEST, preferred_element_type=F32
    )
    branch = iota(factor.shape, 1) == iota(factor.shape, 0) % modes
    factor = jnp.sum(jnp.where(branch, factor, 0.0), axis=1, keepdims=True) * scale
    off = jnp.zeros(owner.shape, jnp.int32)
    for m in range(modes):
        off = jnp.where(rows % modes == m, offsets[0, m], off)
    hit = (rows // modes == cols // HALO) & (off == cols % HALO + 1)
    owner[...] = jnp.where(hit, factor, 0.0)

    row, col = iota((width, width), 0), iota((width, width), 1)
    active = jnp.sum(jnp.where(row == col, mask[...], 0).astype(F32), axis=1, keepdims=True)
    live = jnp.where(active > 0.0, col - row, 2 * width)
    beyond = iota((width, 16), 1)
    source = jnp.where(beyond % 8 < HALO, beyond % 8 - HALO, width + beyond % 8 - HALO)
    gap = jnp.where(active > 0.0, source - iota((width, 16), 0), 2 * width)
    for comp in range(2):
        dif = jnp.where(beyond // 8 == comp, gap, 2 * width)
        for k in range(kd):
            ck = comp * kd + k
            ends = []
            for r in range(rounds):
                p = r * kd + k
                up = [x[p : p + 1, :] for x in emit]
                down = [x[p : p + 1, :] for x in absorb]
                if comp == 1:
                    up, down = down, up
                main[ck, :, r * width : (r + 1) * width] = band(live, up, down).astype(BF16)
                ends.append(band(dif, [x[:, :16] for x in up], [x[:, :16] for x in down]))
            main[ck, :, rounds * width :] = jnp.concatenate(ends, axis=1).astype(BF16)


def sigma_kernel(order, main, green, own, less1, less2, less3, far0, far1, great2, great3, sigma):
    kd, rounds = order.shape
    width = green.shape[2]
    less = (own, less1, less2, less3)
    for k in range(kd):
        index = [order[k, r] for r in range(rounds)]
        ends = jnp.concatenate([x[i, width:] for x, i in zip(less, index)], axis=0)
        for comp in range(2):
            if comp == 0:
                blocks = [x[i, :width] for x, i in zip(less, index)]
            else:
                blocks = [green[1, index[0]]]
                blocks.append(jnp.where(index[1] == 0, far0[...].astype(F32), far1[...].astype(F32)).astype(BF16))
                blocks += [x[i] for x, i in zip((great2, great3), index[2:])]
            weights = main[comp * kd + k]
            acc = dot(weights[:, : rounds * width], jnp.concatenate(blocks, axis=0))
            sigma[comp, k] = (acc + dot(weights[:, rounds * width :], ends)).astype(BF16)


def owner_kernel(got, owner, pol):
    total = jnp.sum(got[...].astype(F32), axis=0)
    pol[...] = dot(owner[...], total, HIGHEST)


def tie(x, y):
    return lax.optimization_barrier((x, y))[0]


def on_device(green, mask, pair_order, q_index, offsets, occupancy, coupling):
    _, kd, width, norb = green.shape
    rounds = pair_order.shape[0]
    count = lax.axis_size(("zl", "c"))
    owned = coupling.shape[0] // lax.axis_size(("x", "y", "zh"))
    mine, order, q_row, spread, mask_row, offset_row, occupancy_row = begin(
        green,
        pair_order[:, 0].T,
        q_index.T,
        coupling.T,
        mask[None, :],
        offsets[None, :],
        occupancy[None, :],
    )
    place = [lax.axis_index(("x", "y", "zh")) * owned, lax.axis_index("c")]
    place = jnp.stack([jnp.asarray(x, jnp.int32) for x in place])[None]

    swap = [(0, 1), (1, 0)]

    def exchange(x):
        near = lax.ppermute(x, "y", [(i, i ^ 1) for i in range(4)])
        return near, lax.ppermute(x, "y", [(i, i ^ 2) for i in range(4)])

    far = lax.ppermute(mine, "zh", swap)
    far = [far[k] for k in range(kd)]
    first, last = green[:, :, :8], green[:, :, width - 8 :]
    masked = first[0] * mask_row[0, None, :8, None].astype(BF16)
    first_core = lax.axis_index("c") == 0

    def edge(x):
        rows = jnp.concatenate([x.reshape(2 * kd, 8, norb), masked], axis=0)
        return rows.reshape(-1, 16, norb)

    from_core = lax.ppermute(edge(jnp.where(first_core, last, first)), "c", swap)
    meet = [(i, i + 1) for i in range(1, count - 1, 2)]
    to_chip = edge(jnp.where(first_core, first, last))
    from_chip = lax.ppermute(to_chip, ("zl", "c"), meet + [(j, i) for i, j in meet])
    onehot, shifted = call(
        shift_kernel,
        "shift",
        (
            shape(coupling.shape[0] * HALO, rounds * kd * HALO),
            shape(kd * HALO, width, norb),
        ),
        [VMEM] * 3,
        (q_row, mask_row, green),
    )
    great = (*far, *exchange(tie(mine, onehot)))
    shifted, first, extended = call(
        halo_kernel,
        "halo",
        (
            shape(*shifted.shape),
            shape(kd * HALO, norb, dtype=F32),
            shape(kd, width + 16, norb),
        ),
        [VMEM] * 6,
        (order, place, green, shifted, from_core, from_chip),
    )
    dense = call(
        terms_kernel,
        "terms",
        shape(onehot.shape[0], norb),
        [VMEM] * 8,
        (order, *great, shifted, first, onehot),
        scratch=[pltpu.VMEM((onehot.shape[0], norb), BF16), pltpu.SemaphoreType.DMA((PIECES,))],
        out_specs=pl.BlockSpec(memory_space=pl.ANY),
    )
    less = (lax.ppermute(extended, "zh", swap), *exchange(tie(extended, dense)))
    got = lax.all_to_all(dense.reshape(16, -1, norb), ("x", "y"), 0, 0, tiled=True)
    sent = call(
        column_kernel, "column", shape(2 * count, owned * HALO, norb), [VMEM], (got,)
    )
    got = lax.all_to_all(sent, ("c", "zh", "zl"), 0, 0, tiled=True)

    main, owner = call(
        functools.partial(weights_kernel, scale=1.0 / (width * count)),
        "weights",
        (
            shape(2 * kd, width, rounds * (width + 16)),
            shape(owned * offsets.shape[0], owned * HALO, dtype=F32),
        ),
        [SMEM] * 4 + [VMEM] * 2,
        (q_row, place, offset_row, occupancy_row, tie(spread, sent), mask_row),
    )
    sigma = call(
        sigma_kernel,
        "sigma",
        shape(*green.shape),
        [SMEM] + [VMEM] * 10,
        (order, main, green, extended, *less, *great),
        flops=2**34,
    )
    pol = call(
        owner_kernel,
        "owner",
        shape(owner.shape[0], norb, dtype=F32),
        [VMEM] * 2,
        (got, owner),
    )
    return sigma, pol.reshape(owned, -1, norb)


def solution(mesh):
    split = Mesh(mesh.devices.reshape(4, 4, 2, 4, 2), AXES)
    mom, en = ("x", "y", "zh"), ("zl", "c")
    in_specs = (P(None, mom, en, None), P(en), P(None, mom, None), P(None, mom), P(), P(), P())
    out_specs = (P(None, mom, en, None), P(mom, None, None))
    return jax.shard_map(
        on_device, mesh=split, in_specs=in_specs, out_specs=out_specs, check_vma=False
    )
```

```python
import functools

import jax
import jax.numpy as jnp
from jax import lax
from jax.experimental import pallas as pl
from jax.experimental.pallas import tpu as pltpu
from jax.sharding import Mesh, PartitionSpec as P

HALO = 4
AXES = ("x", "y", "zh", "zl", "c")
F32 = jnp.float32
PIECES = 4
BF16 = jnp.bfloat16
HIGHEST = lax.Precision.HIGHEST
SMEM = pl.BlockSpec(memory_space=pltpu.SMEM)
LIMIT = 12 * 1024 * 1024
BEGIN_LIMIT = 12 * 1024 * 1024
VMEM = pl.BlockSpec(memory_space=pltpu.VMEM)


def iota(shape, dim):
    return lax.broadcasted_iota(jnp.int32, shape, dim)


def dot(a, b, precision=None):
    return lax.dot_general(
        a, b, (((1,), (0,)), ((), ())), precision=precision, preferred_element_type=F32
    )


def band(dif, above, below):
    out = jnp.zeros(dif.shape, F32)
    for d in range(1, HALO + 1):
        out = jnp.where(dif == d, above[d - 1], out)
        out = jnp.where(dif == -d, below[d - 1], out)
    return out


def pair_products(great, shifted, k):
    return [
        jnp.sum(great * shifted[k * HALO + d].astype(F32), axis=0, keepdims=True)
        for d in range(HALO)
    ]


def entry(table, i, j):
    return table[i : i + 1, j : j + 1]


def choose(blocks, index):
    low, high = blocks[0][...].astype(F32), blocks[1][...].astype(F32)
    return jnp.where(jnp.broadcast_to(index, low.shape) == 0, low, high)


def call(kernel, name, outs, specs, args, scratch=(), flops=2**20, out_specs=None):
    return pl.pallas_call(
        kernel,
        out_shape=outs,
        in_specs=specs,
        out_specs=out_specs or jax.tree.map(lambda _: VMEM, outs),
        scratch_shapes=scratch,
        compiler_params=pltpu.CompilerParams(vmem_limit_bytes=LIMIT),
        cost_estimate=pl.CostEstimate(flops=flops, bytes_accessed=2**20, transcendentals=0),
        name=name,
    )(*args)


def shape(*dims, dtype=BF16):
    return jax.ShapeDtypeStruct(dims, dtype)


def begin_kernel(green, *refs):
    count = (len(refs) - 2) // 2
    small, great, kept, sems = refs[:count], refs[count], refs[count + 1 : -1], refs[-1]
    pairs = list(zip(small, kept))
    for k in range(great.shape[0]):
        pairs.append((green.at[1, k], great.at[k]))
    copies = [pltpu.make_async_copy(a, b, sems.at[i]) for i, (a, b) in enumerate(pairs)]
    for copy in reversed(copies):
        copy.start()
    for copy in copies:
        copy.wait()


def begin(green, *small):
    anywhere = pl.BlockSpec(memory_space=pltpu.HBM)
    _, kd, width, norb = green.shape
    outs = [shape(kd, width, norb)] + [shape(*x.shape, dtype=x.dtype) for x in small]
    green, *small = [pltpu.with_memory_space_constraint(x, pltpu.HBM) for x in (green, *small)]
    return pl.pallas_call(
        begin_kernel,
        out_shape=outs,
        in_specs=[anywhere] * (1 + len(small)),
        out_specs=[VMEM] * len(outs),
        scratch_shapes=[pltpu.SemaphoreType.DMA((len(small) + kd,))],
        compiler_params=pltpu.CompilerParams(vmem_limit_bytes=BEGIN_LIMIT),
        cost_estimate=pl.CostEstimate(flops=0, bytes_accessed=2**18, transcendentals=0),
        name="begin",
    )(green, *small)


def shift_kernel(q_row, mask, green, onehot, shifted):
    kd, rounds = q_row.shape
    width = mask.shape[1]
    goal = jnp.zeros((1, onehot.shape[1]), jnp.int32)
    lane = iota(goal.shape, 1)
    for p in range(rounds * kd):
        goal = jnp.where(lane // HALO == p, entry(q_row, p % kd, p // kd) * HALO + lane % HALO, goal)
    onehot[...] = (iota(onehot.shape, 0) == goal).astype(F32).astype(BF16)

    row, col = iota((width, width), 0), iota((width, width), 1)
    weights = jnp.broadcast_to(mask[...], (width, width)).astype(F32)
    for d in range(1, HALO + 1):
        move = jnp.where(col == row + d, weights, 0.0).astype(BF16)
        for k in range(kd):
            shifted[k * HALO + d - 1] = dot(move, green[0, k]).astype(BF16)


def halo_kernel(order, place, green, shifted, from_core, from_chip, full, first, extended):
    kd, width = green.shape[1:3]
    first_core = jnp.broadcast_to(entry(place, 0, 1)[None], from_core.shape) == 0
    core, chip = from_core[...].astype(F32), from_chip[...].astype(F32)
    before = jnp.where(first_core, chip, core).astype(BF16)
    after = jnp.where(first_core, core, chip).astype(BF16)
    size = before.shape[0] * before.shape[1]
    before, after = before.reshape(size, -1), after.reshape(size, -1)
    both = jnp.concatenate([before, after], axis=0)
    rows, cols = iota((16, size), 0), iota((16, size), 1)
    row, col = iota((16, 2 * size), 0), iota((16, 2 * size), 1)
    kind = row // HALO
    source = kind // 2 * 8 * kd + kind % 2 * size + (1 - kind % 2) * (8 - HALO) + row % HALO
    for k in range(kd):
        for d in range(1, HALO + 1):
            at = k * HALO + d - 1
            wrap = (rows + d >= 16) & (cols == rows + d - 16 + (2 * kd + k) * 8)
            moved = dot(wrap.astype(F32).astype(BF16), after)
            full[at, : width - 16] = shifted[at, : width - 16]
            full[at, width - 16 :] = (shifted[at, width - 16 :].astype(F32) + moved).astype(BF16)
        extended[k, :width] = green[0, k]
        pick = (col == source + 8 * k).astype(F32).astype(BF16)
        extended[k, width:] = dot(pick, both).astype(BF16)
    lines = []
    for k in range(kd):
        lines += pair_products(choose(green.at[1], entry(order, k, 0)), full, k)
    first[...] = jnp.concatenate(lines, axis=0)


def terms_kernel(order, far0, far1, near, next_near, shifted, first, onehot, out, held, sems):
    lines = [first[...]]
    far = (far0, far1)
    for r, ref in ((1, far), (2, near), (3, next_near)):
        for k in range(len(far)):
            lines += pair_products(choose(ref, entry(order, k, r)), shifted, k)
    terms = jnp.concatenate(lines, axis=0).astype(BF16)
    step = out.shape[0] // PIECES
    copies = []
    for i in range(PIECES):
        rows = pl.ds(i * step, step)
        held[rows] = dot(onehot[rows], terms).astype(BF16)
        copies.append(pltpu.make_async_copy(held.at[rows], out.at[rows], sems.at[i]))
        copies[-1].start()
    for copy in copies:
        copy.wait()


def column_kernel(got, out):
    total = jnp.sum(got[...].astype(F32), axis=0).astype(BF16)
    half = out.shape[1]
    for dest in range(out.shape[0]):
        at = dest // (out.shape[0] // 4) % 2 * half
        out[dest] = total[at : at + half]


def weights_kernel(q_row, place, offsets, occupancy, coupling, mask, main, owner, *, scale):
    kd, rounds = q_row.shape
    width = mask.shape[1]
    modes = coupling.shape[0]
    pairs = rounds * kd

    q_col = jnp.zeros((pairs, coupling.shape[1]), jnp.int32)
    for p in range(pairs):
        q_col = jnp.where(iota(q_col.shape, 0) == p, q_row[p % kd, p // kd], q_col)
    chosen = (q_col == iota(q_col.shape, 1)).astype(F32)
    strength = lax.dot_general(
        chosen, coupling[...], (((1,), (1,)), ((), ())), precision=HIGHEST, preferred_element_type=F32
    )
    off_col = jnp.zeros((modes, width), jnp.int32)
    occ_col = jnp.zeros((modes, width), F32)
    for m in range(modes):
        off_col = jnp.where(iota(off_col.shape, 0) == m, offsets[0, m], off_col)
        occ_col = jnp.where(iota(off_col.shape, 0) == m, occupancy[0, m], occ_col)
    emit, absorb = [], []
    for d in range(1, HALO + 1):
        emit.append(dot(strength, jnp.where(off_col == d, occ_col + 1.0, 0.0), HIGHEST))
        absorb.append(dot(strength, jnp.where(off_col == d, occ_col, 0.0), HIGHEST))

    rows, cols = iota(owner.shape, 0), iota(owner.shape, 1)
    wide = (owner.shape[0], coupling.shape[1])
    mine = (iota(wide, 1) == place[0, 0] + iota(wide, 0) // modes).astype(F32)
    factor = lax.dot_general(
        mine, coupling[...], (((1,), (1,)), ((), ())), precision=HIGHEST, preferred_element_type=F32
    )
    branch = iota(factor.shape, 1) == iota(factor.shape, 0) % modes
    factor = jnp.sum(jnp.where(branch, factor, 0.0), axis=1, keepdims=True) * scale
    off = jnp.zeros(owner.shape, jnp.int32)
    for m in range(modes):
        off = jnp.where(rows % modes == m, offsets[0, m], off)
    hit = (rows // modes == cols // HALO) & (off == cols % HALO + 1)
    owner[...] = jnp.where(hit, factor, 0.0)

    row, col = iota((width, width), 0), iota((width, width), 1)
    active = jnp.sum(jnp.where(row == col, mask[...], 0).astype(F32), axis=1, keepdims=True)
    live = jnp.where(active > 0.0, col - row, 2 * width)
    beyond = iota((width, 16), 1)
    source = jnp.where(beyond % 8 < HALO, beyond % 8 - HALO, width + beyond % 8 - HALO)
    gap = jnp.where(active > 0.0, source - iota((width, 16), 0), 2 * width)
    for comp in range(2):
        dif = jnp.where(beyond // 8 == comp, gap, 2 * width)
        for k in range(kd):
            ck = comp * kd + k
            ends = []
            for r in range(rounds):
                p = r * kd + k
                up = [x[p : p + 1, :] for x in emit]
                down = [x[p : p + 1, :] for x in absorb]
                if comp == 1:
                    up, down = down, up
                main[ck, :, r * width : (r + 1) * width] = band(live, up, down).astype(BF16)
                ends.append(band(dif, [x[:, :16] for x in up], [x[:, :16] for x in down]))
            main[ck, :, rounds * width :] = jnp.concatenate(ends, axis=1).astype(BF16)


def sigma_kernel(order, main, green, own, less1, less2, less3, far0, far1, great2, great3, sigma):
    kd, rounds = order.shape
    width = green.shape[2]
    less = (own, less1, less2, less3)
    for k in range(kd):
        index = [order[k, r] for r in range(rounds)]
        ends = jnp.concatenate([x[i, width:] for x, i in zip(less, index)], axis=0)
        for comp in range(2):
            if comp == 0:
                blocks = [x[i, :width] for x, i in zip(less, index)]
            else:
                blocks = [green[1, index[0]]]
                blocks.append(jnp.where(index[1] == 0, far0[...].astype(F32), far1[...].astype(F32)).astype(BF16))
                blocks += [x[i] for x, i in zip((great2, great3), index[2:])]
            weights = main[comp * kd + k]
            acc = dot(weights[:, : rounds * width], jnp.concatenate(blocks, axis=0))
            sigma[comp, k] = (acc + dot(weights[:, rounds * width :], ends)).astype(BF16)


def owner_kernel(got, owner, pol):
    total = jnp.sum(got[...].astype(F32), axis=0)
    pol[...] = dot(owner[...], total, HIGHEST)


def tie(x, y):
    return lax.optimization_barrier((x, y))[0]


def on_device(green, mask, pair_order, q_index, offsets, occupancy, coupling):
    _, kd, width, norb = green.shape
    rounds = pair_order.shape[0]
    count = lax.axis_size(("zl", "c"))
    owned = coupling.shape[0] // lax.axis_size(("x", "y", "zh"))
    mine, order, q_row, mask_row = begin(green, pair_order[:, 0].T, q_index.T, mask[None, :])
    spread, offset_row, occupancy_row = coupling.T, offsets[None, :], occupancy[None, :]
    place = [lax.axis_index(("x", "y", "zh")) * owned, lax.axis_index("c")]
    place = jnp.stack([jnp.asarray(x, jnp.int32) for x in place])[None]

    swap = [(0, 1), (1, 0)]

    def exchange(x):
        near = lax.ppermute(x, "y", [(i, i ^ 1) for i in range(4)])
        return near, lax.ppermute(x, "y", [(i, i ^ 2) for i in range(4)])

    far = lax.ppermute(mine, "zh", swap)
    far = [far[k] for k in range(kd)]
    first, last = green[:, :, :8], green[:, :, width - 8 :]
    masked = first[0] * mask_row[0, None, :8, None].astype(BF16)
    first_core = lax.axis_index("c") == 0

    def edge(x):
        rows = jnp.concatenate([x.reshape(2 * kd, 8, norb), masked], axis=0)
        return rows.reshape(-1, 16, norb)

    from_core = lax.ppermute(edge(jnp.where(first_core, last, first)), "c", swap)
    meet = [(i, i + 1) for i in range(1, count - 1, 2)]
    to_chip = edge(jnp.where(first_core, first, last))
    from_chip = lax.ppermute(to_chip, ("zl", "c"), meet + [(j, i) for i, j in meet])
    onehot, shifted = call(
        shift_kernel,
        "shift",
        (
            shape(coupling.shape[0] * HALO, rounds * kd * HALO),
            shape(kd * HALO, width, norb),
        ),
        [VMEM] * 3,
        (q_row, mask_row, green),
    )
    great = (*far, *exchange(tie(mine, onehot)))
    shifted, first, extended = call(
        halo_kernel,
        "halo",
        (
            shape(*shifted.shape),
            shape(kd * HALO, norb, dtype=F32),
            shape(kd, width + 16, norb),
        ),
        [VMEM] * 6,
        (order, place, green, shifted, from_core, from_chip),
    )
    dense = call(
        terms_kernel,
        "terms",
        shape(onehot.shape[0], norb),
        [VMEM] * 8,
        (order, *great, shifted, first, onehot),
        scratch=[pltpu.VMEM((onehot.shape[0], norb), BF16), pltpu.SemaphoreType.DMA((PIECES,))],
        out_specs=pl.BlockSpec(memory_space=pl.ANY),
    )
    less = (lax.ppermute(extended, "zh", swap), *exchange(tie(extended, dense)))
    got = lax.all_to_all(dense.reshape(16, -1, norb), ("x", "y"), 0, 0, tiled=True)
    sent = call(
        column_kernel, "column", shape(2 * count, owned * HALO, norb), [VMEM], (got,)
    )
    got = lax.all_to_all(sent, ("c", "zh", "zl"), 0, 0, tiled=True)

    main, owner = call(
        functools.partial(weights_kernel, scale=1.0 / (width * count)),
        "weights",
        (
            shape(2 * kd, width, rounds * (width + 16)),
            shape(owned * offsets.shape[0], owned * HALO, dtype=F32),
        ),
        [SMEM] * 4 + [VMEM] * 2,
        (q_row, place, offset_row, occupancy_row, tie(spread, sent), mask_row),
    )
    sigma = call(
        sigma_kernel,
        "sigma",
        shape(*green.shape),
        [SMEM] + [VMEM] * 10,
        (order, main, green, extended, *less, *great),
        flops=2**34,
    )
    pol = call(
        owner_kernel,
        "owner",
        shape(owner.shape[0], norb, dtype=F32),
        [VMEM] * 2,
        (got, owner),
    )
    return sigma, pol.reshape(owned, -1, norb)


def solution(mesh):
    split = Mesh(mesh.devices.reshape(4, 4, 2, 4, 2), AXES)
    mom, en = ("x", "y", "zh"), ("zl", "c")
    in_specs = (P(None, mom, en, None), P(en), P(None, mom, None), P(None, mom), P(), P(), P())
    out_specs = (P(None, mom, en, None), P(mom, None, None))
    return jax.shard_map(
        on_device, mesh=split, in_specs=in_specs, out_specs=out_specs, check_vma=False
    )
```

```python
import functools

import jax
import jax.numpy as jnp
from jax import lax
from jax.experimental import pallas as pl
from jax.experimental.pallas import tpu as pltpu
from jax.sharding import Mesh, PartitionSpec as P

HALO = 4
AXES = ("x", "y", "zh", "zl", "c")
F32 = jnp.float32
PIECES = 4
BF16 = jnp.bfloat16
HIGHEST = lax.Precision.HIGHEST
SMEM = pl.BlockSpec(memory_space=pltpu.SMEM)
LIMIT = 12 * 1024 * 1024
BEGIN_LIMIT = 12 * 1024 * 1024
VMEM = pl.BlockSpec(memory_space=pltpu.VMEM)


def iota(shape, dim):
    return lax.broadcasted_iota(jnp.int32, shape, dim)


def dot(a, b, precision=None):
    return lax.dot_general(
        a, b, (((1,), (0,)), ((), ())), precision=precision, preferred_element_type=F32
    )


def band(dif, above, below):
    out = jnp.zeros(dif.shape, F32)
    for d in range(1, HALO + 1):
        out = jnp.where(dif == d, above[d - 1], out)
        out = jnp.where(dif == -d, below[d - 1], out)
    return out


def pair_products(great, shifted, k):
    return [
        jnp.sum(great * shifted[k * HALO + d].astype(F32), axis=0, keepdims=True)
        for d in range(HALO)
    ]


def entry(table, i, j):
    return table[i : i + 1, j : j + 1]


def choose(blocks, index):
    low, high = blocks[0][...].astype(F32), blocks[1][...].astype(F32)
    return jnp.where(jnp.broadcast_to(index, low.shape) == 0, low, high)


def call(kernel, name, outs, specs, args, scratch=(), flops=2**20, out_specs=None):
    return pl.pallas_call(
        kernel,
        out_shape=outs,
        in_specs=specs,
        out_specs=out_specs or jax.tree.map(lambda _: VMEM, outs),
        scratch_shapes=scratch,
        compiler_params=pltpu.CompilerParams(vmem_limit_bytes=LIMIT),
        cost_estimate=pl.CostEstimate(flops=flops, bytes_accessed=2**20, transcendentals=0),
        name=name,
    )(*args)


def shape(*dims, dtype=BF16):
    return jax.ShapeDtypeStruct(dims, dtype)


def begin_kernel(green, *refs):
    count = (len(refs) - 2) // 2
    small, great, kept, sems = refs[:count], refs[count], refs[count + 1 : -1], refs[-1]
    pairs = list(zip(small, kept))
    for k in range(great.shape[0]):
        pairs.append((green.at[1, k], great.at[k]))
    copies = [pltpu.make_async_copy(a, b, sems.at[i]) for i, (a, b) in enumerate(pairs)]
    for copy in reversed(copies):
        copy.start()
    for copy in copies:
        copy.wait()


def begin(green, *small):
    anywhere = pl.BlockSpec(memory_space=pltpu.HBM)
    _, kd, width, norb = green.shape
    outs = [shape(kd, width, norb)] + [shape(*x.shape, dtype=x.dtype) for x in small]
    green, *small = [pltpu.with_memory_space_constraint(x, pltpu.HBM) for x in (green, *small)]
    return pl.pallas_call(
        begin_kernel,
        out_shape=outs,
        in_specs=[anywhere] * (1 + len(small)),
        out_specs=[VMEM] * len(outs),
        scratch_shapes=[pltpu.SemaphoreType.DMA((len(small) + kd,))],
        compiler_params=pltpu.CompilerParams(vmem_limit_bytes=BEGIN_LIMIT),
        cost_estimate=pl.CostEstimate(flops=0, bytes_accessed=2**18, transcendentals=0),
        name="begin",
    )(green, *small)


def shift_kernel(q_row, mask, green, onehot, shifted):
    kd, rounds = q_row.shape
    width = mask.shape[1]
    goal = jnp.zeros((1, onehot.shape[1]), jnp.int32)
    lane = iota(goal.shape, 1)
    for p in range(rounds * kd):
        goal = jnp.where(lane // HALO == p, entry(q_row, p % kd, p // kd) * HALO + lane % HALO, goal)
    onehot[...] = (iota(onehot.shape, 0) == goal).astype(F32).astype(BF16)

    row, col = iota((width, width), 0), iota((width, width), 1)
    weights = jnp.broadcast_to(mask[...], (width, width)).astype(F32)
    for d in range(1, HALO + 1):
        move = jnp.where(col == row + d, weights, 0.0).astype(BF16)
        for k in range(kd):
            shifted[k * HALO + d - 1] = dot(move, green[0, k]).astype(BF16)


def halo_kernel(order, place, green, shifted, from_core, from_chip, full, first, extended):
    kd, width = green.shape[1:3]
    first_core = jnp.broadcast_to(entry(place, 0, 1)[None], from_core.shape) == 0
    core, chip = from_core[...].astype(F32), from_chip[...].astype(F32)
    before = jnp.where(first_core, chip, core).astype(BF16)
    after = jnp.where(first_core, core, chip).astype(BF16)
    size = before.shape[0] * before.shape[1]
    before, after = before.reshape(size, -1), after.reshape(size, -1)
    both = jnp.concatenate([before, after], axis=0)
    rows, cols = iota((16, size), 0), iota((16, size), 1)
    row, col = iota((16, 2 * size), 0), iota((16, 2 * size), 1)
    kind = row // HALO
    source = kind // 2 * 8 * kd + kind % 2 * size + (1 - kind % 2) * (8 - HALO) + row % HALO
    for k in range(kd):
        for d in range(1, HALO + 1):
            at = k * HALO + d - 1
            wrap = (rows + d >= 16) & (cols == rows + d - 16 + (2 * kd + k) * 8)
            moved = dot(wrap.astype(F32).astype(BF16), after)
            full[at, : width - 16] = shifted[at, : width - 16]
            full[at, width - 16 :] = (shifted[at, width - 16 :].astype(F32) + moved).astype(BF16)
        extended[k, :width] = green[0, k]
        pick = (col == source + 8 * k).astype(F32).astype(BF16)
        extended[k, width:] = dot(pick, both).astype(BF16)
    lines = []
    for k in range(kd):
        lines += pair_products(choose(green.at[1], entry(order, k, 0)), full, k)
    first[...] = jnp.concatenate(lines, axis=0)


def terms_kernel(order, far0, far1, near, next_near, shifted, first, onehot, out, held, sems):
    lines = [first[...]]
    far = (far0, far1)
    for r, ref in ((1, far), (2, near), (3, next_near)):
        for k in range(len(far)):
            lines += pair_products(choose(ref, entry(order, k, r)), shifted, k)
    terms = jnp.concatenate(lines, axis=0).astype(BF16)
    step = out.shape[0] // PIECES
    copies = []
    for i in range(PIECES):
        rows = pl.ds(i * step, step)
        held[rows] = dot(onehot[rows], terms).astype(BF16)
        copies.append(pltpu.make_async_copy(held.at[rows], out.at[rows], sems.at[i]))
        copies[-1].start()
    for copy in copies:
        copy.wait()


def column_kernel(got, out):
    total = jnp.sum(got[...].astype(F32), axis=0).astype(BF16)
    half = out.shape[1]
    for dest in range(out.shape[0]):
        at = dest // (out.shape[0] // 4) % 2 * half
        out[dest] = total[at : at + half]


def weights_kernel(q_row, place, offsets, occupancy, coupling, mask, main, owner, *, scale):
    kd, rounds = q_row.shape
    width = mask.shape[1]
    modes = coupling.shape[0]
    pairs = rounds * kd

    q_col = jnp.zeros((pairs, coupling.shape[1]), jnp.int32)
    for p in range(pairs):
        q_col = jnp.where(iota(q_col.shape, 0) == p, q_row[p % kd, p // kd], q_col)
    chosen = (q_col == iota(q_col.shape, 1)).astype(F32)
    strength = lax.dot_general(
        chosen, coupling[...], (((1,), (1,)), ((), ())), precision=HIGHEST, preferred_element_type=F32
    )
    off_col = jnp.zeros((modes, width), jnp.int32)
    occ_col = jnp.zeros((modes, width), F32)
    for m in range(modes):
        off_col = jnp.where(iota(off_col.shape, 0) == m, offsets[0, m], off_col)
        occ_col = jnp.where(iota(off_col.shape, 0) == m, occupancy[0, m], occ_col)
    emit, absorb = [], []
    for d in range(1, HALO + 1):
        emit.append(dot(strength, jnp.where(off_col == d, occ_col + 1.0, 0.0), HIGHEST))
        absorb.append(dot(strength, jnp.where(off_col == d, occ_col, 0.0), HIGHEST))

    rows, cols = iota(owner.shape, 0), iota(owner.shape, 1)
    wide = (owner.shape[0], coupling.shape[1])
    mine = (iota(wide, 1) == place[0, 0] + iota(wide, 0) // modes).astype(F32)
    factor = lax.dot_general(
        mine, coupling[...], (((1,), (1,)), ((), ())), precision=HIGHEST, preferred_element_type=F32
    )
    branch = iota(factor.shape, 1) == iota(factor.shape, 0) % modes
    factor = jnp.sum(jnp.where(branch, factor, 0.0), axis=1, keepdims=True) * scale
    off = jnp.zeros(owner.shape, jnp.int32)
    for m in range(modes):
        off = jnp.where(rows % modes == m, offsets[0, m], off)
    hit = (rows // modes == cols // HALO) & (off == cols % HALO + 1)
    owner[...] = jnp.where(hit, factor, 0.0)

    row, col = iota((width, width), 0), iota((width, width), 1)
    active = jnp.sum(jnp.where(row == col, mask[...], 0).astype(F32), axis=1, keepdims=True)
    live = jnp.where(active > 0.0, col - row, 2 * width)
    beyond = iota((width, 16), 1)
    source = jnp.where(beyond % 8 < HALO, beyond % 8 - HALO, width + beyond % 8 - HALO)
    gap = jnp.where(active > 0.0, source - iota((width, 16), 0), 2 * width)
    for comp in range(2):
        dif = jnp.where(beyond // 8 == comp, gap, 2 * width)
        for k in range(kd):
            ck = comp * kd + k
            ends = []
            for r in range(rounds):
                p = r * kd + k
                up = [x[p : p + 1, :] for x in emit]
                down = [x[p : p + 1, :] for x in absorb]
                if comp == 1:
                    up, down = down, up
                main[ck, :, r * width : (r + 1) * width] = band(live, up, down).astype(BF16)
                ends.append(band(dif, [x[:, :16] for x in up], [x[:, :16] for x in down]))
            main[ck, :, rounds * width :] = jnp.concatenate(ends, axis=1).astype(BF16)


def sigma_kernel(order, main, green, own, less1, less2, less3, far0, far1, great2, great3, sigma):
    kd, rounds = order.shape
    width = green.shape[2]
    less = (own, less1, less2, less3)
    for k in range(kd):
        index = [order[k, r] for r in range(rounds)]
        ends = jnp.concatenate([x[i, width:] for x, i in zip(less, index)], axis=0)
        for comp in range(2):
            if comp == 0:
                blocks = [x[i, :width] for x, i in zip(less, index)]
            else:
                blocks = [green[1, index[0]]]
                blocks.append(jnp.where(index[1] == 0, far0[...].astype(F32), far1[...].astype(F32)).astype(BF16))
                blocks += [x[i] for x, i in zip((great2, great3), index[2:])]
            weights = main[comp * kd + k]
            acc = dot(weights[:, : rounds * width], jnp.concatenate(blocks, axis=0))
            sigma[comp, k] = (acc + dot(weights[:, rounds * width :], ends)).astype(BF16)


def owner_kernel(got, owner, pol):
    total = jnp.sum(got[...].astype(F32), axis=0)
    high, top = owner[...].astype(BF16), total.astype(BF16)
    low = (owner[...] - high.astype(F32)).astype(BF16)
    rest = (total - top.astype(F32)).astype(BF16)
    pol[...] = dot(high, top) + (dot(high, rest) + dot(low, top))


def tie(x, y):
    return lax.optimization_barrier((x, y))[0]


def on_device(green, mask, pair_order, q_index, offsets, occupancy, coupling):
    _, kd, width, norb = green.shape
    rounds = pair_order.shape[0]
    count = lax.axis_size(("zl", "c"))
    owned = coupling.shape[0] // lax.axis_size(("x", "y", "zh"))
    mine, order, q_row, mask_row = begin(green, pair_order[:, 0].T, q_index.T, mask[None, :])
    spread, offset_row, occupancy_row = coupling.T, offsets[None, :], occupancy[None, :]
    place = [lax.axis_index(("x", "y", "zh")) * owned, lax.axis_index("c")]
    place = jnp.stack([jnp.asarray(x, jnp.int32) for x in place])[None]

    swap = [(0, 1), (1, 0)]

    def exchange(x):
        near = lax.ppermute(x, "y", [(i, i ^ 1) for i in range(4)])
        return near, lax.ppermute(x, "y", [(i, i ^ 2) for i in range(4)])

    far = lax.ppermute(mine, "zh", swap)
    far = [far[k] for k in range(kd)]
    first, last = green[:, :, :8], green[:, :, width - 8 :]
    masked = first[0] * mask_row[0, None, :8, None].astype(BF16)
    first_core = lax.axis_index("c") == 0

    def edge(x):
        rows = jnp.concatenate([x.reshape(2 * kd, 8, norb), masked], axis=0)
        return rows.reshape(-1, 16, norb)

    from_core = lax.ppermute(edge(jnp.where(first_core, last, first)), "c", swap)
    meet = [(i, i + 1) for i in range(1, count - 1, 2)]
    to_chip = edge(jnp.where(first_core, first, last))
    from_chip = lax.ppermute(to_chip, ("zl", "c"), meet + [(j, i) for i, j in meet])
    onehot, shifted = call(
        shift_kernel,
        "shift",
        (
            shape(coupling.shape[0] * HALO, rounds * kd * HALO),
            shape(kd * HALO, width, norb),
        ),
        [VMEM] * 3,
        (q_row, mask_row, green),
    )
    great = (*far, *exchange(tie(mine, onehot)))
    shifted, first, extended = call(
        halo_kernel,
        "halo",
        (
            shape(*shifted.shape),
            shape(kd * HALO, norb, dtype=F32),
            shape(kd, width + 16, norb),
        ),
        [VMEM] * 6,
        (order, place, green, shifted, from_core, from_chip),
    )
    dense = call(
        terms_kernel,
        "terms",
        shape(onehot.shape[0], norb),
        [VMEM] * 8,
        (order, *great, shifted, first, onehot),
        scratch=[pltpu.VMEM((onehot.shape[0], norb), BF16), pltpu.SemaphoreType.DMA((PIECES,))],
        out_specs=pl.BlockSpec(memory_space=pl.ANY),
    )
    less = (lax.ppermute(extended, "zh", swap), *exchange(tie(extended, dense)))
    got = lax.all_to_all(dense.reshape(16, -1, norb), ("x", "y"), 0, 0, tiled=True)
    sent = call(
        column_kernel, "column", shape(2 * count, owned * HALO, norb), [VMEM], (got,)
    )
    got = lax.all_to_all(sent, ("c", "zh", "zl"), 0, 0, tiled=True)

    main, owner = call(
        functools.partial(weights_kernel, scale=1.0 / (width * count)),
        "weights",
        (
            shape(2 * kd, width, rounds * (width + 16)),
            shape(owned * offsets.shape[0], owned * HALO, dtype=F32),
        ),
        [SMEM] * 4 + [VMEM] * 2,
        (q_row, place, offset_row, occupancy_row, tie(spread, sent), mask_row),
    )
    sigma = call(
        sigma_kernel,
        "sigma",
        shape(*green.shape),
        [SMEM] + [VMEM] * 10,
        (order, main, green, extended, *less, *great),
        flops=2**34,
    )
    pol = call(
        owner_kernel,
        "owner",
        shape(owner.shape[0], norb, dtype=F32),
        [VMEM] * 2,
        (got, owner),
    )
    return sigma, pol.reshape(owned, -1, norb)


def solution(mesh):
    split = Mesh(mesh.devices.reshape(4, 4, 2, 4, 2), AXES)
    mom, en = ("x", "y", "zh"), ("zl", "c")
    in_specs = (P(None, mom, en, None), P(en), P(None, mom, None), P(None, mom), P(), P(), P())
    out_specs = (P(None, mom, en, None), P(mom, None, None))
    return jax.shard_map(
        on_device, mesh=split, in_specs=in_specs, out_specs=out_specs, check_vma=False
    )
```
